256 devices in a mesh: dp: 64 (over y_hi, z, x), mp: 4 (over y_lo, core).
Axes of the slice: x: 4, y: 4 (y_hi: 2, y_lo: 2; y = y_hi * 2 + y_lo), z: 8, core: 2. Of those that a mesh axis runs over, the one named last changes fastest.
Arguments:
- image_emb: bfloat16 [65536, 1024], P('dp', 'mp'), may hold values from -1 to 1
- text_emb: bfloat16 [65536, 1024], P('dp', 'mp'), may hold values from -1 to 1
- logit_scale: float32 [1], replicated, may hold values from 60 to 100
Outputs:
- image_grad: bfloat16 [65536, 1024], P('dp', 'mp')
- text_grad: bfloat16 [65536, 1024], P('dp', 'mp')
- pair_loss: float32 [65536], P(('dp', 'mp'))
The draws below stay inside these ranges and needn't reach their ends.
All inputs are finite; a program needn't handle non-finite values.
Results may differ from the reference program's by a relative error of at most 0.0041.
Values may be sent and summed in bfloat16 or wider, within the bound.
A program may use at most 64 MiB of HBM per device.

```python
import jax
import jax.numpy as jnp
from jax import lax

WIDTH = 1024
ROWS = 1024
PAIRS = 65536
N_DP = 64


def common_part(key):
    return jax.random.normal(key, (PAIRS, WIDTH), jnp.float32)


def draw_image_emb(key, part):
    shared = common_part(key)
    key = jax.random.fold_in(key, 11)
    own_key = jax.random.fold_in(key, 0)
    own_noise = jax.random.normal(own_key, (PAIRS, WIDTH), jnp.float32)
    drawn_rows = 0.316 * shared + 0.949 * own_noise
    result = drawn_rows
    return jnp.clip(result / jnp.sqrt(WIDTH * 1.0), -1.0, 1.0).astype(jnp.bfloat16)


def draw_text_emb(key, part):
    shared = common_part(key)
    key = jax.random.fold_in(key, 12)
    own_key = jax.random.fold_in(key, 0)
    own_noise = jax.random.normal(own_key, (PAIRS, WIDTH), jnp.float32)
    drawn_rows = 0.316 * shared + 0.949 * own_noise
    result = drawn_rows
    return jnp.clip(result / jnp.sqrt(WIDTH * 1.0), -1.0, 1.0).astype(jnp.bfloat16)


def setup_inputs(seed: int = 0) -> dict:
    seeds = jax.random.split(jax.random.key(seed), 4)
    image_emb = draw_image_emb(jax.random.fold_in(seeds[3], 71), 0)
    text_emb = draw_text_emb(jax.random.fold_in(seeds[3], 71), 0)
    logit_scale = jnp.clip(jax.random.uniform(seeds[2], (1,), jnp.float32, 60.0, 100.0), 60.0, 100.0)
    return {"image_emb": image_emb, "text_emb": text_emb, "logit_scale": logit_scale}


def score_tile(left_rows, right_rows, factor):
    return factor * jnp.dot(left_rows, right_rows.T, preferred_element_type=jnp.float32)


def reference(image_emb, text_emb, logit_scale):
    factor = logit_scale[0]
    image_blocks = image_emb.reshape(N_DP, ROWS, WIDTH)
    text_blocks = text_emb.reshape(N_DP, ROWS, WIDTH)
    prev_blocks = jnp.roll(text_blocks, 1, axis=0)
    identity = (jnp.arange(ROWS)[:, None] == jnp.arange(ROWS)[None, :]).astype(jnp.float32)

    def statistics(block):
        left_rows, own_text, prev_text = block
        score_own = score_tile(left_rows, own_text, factor)
        score_prev = score_tile(left_rows, prev_text, factor)
        row_lse = jax.nn.logsumexp(jnp.concatenate([score_own, score_prev], axis=1), axis=1)
        own_part = jax.nn.logsumexp(score_own, axis=0)
        prev_part = jax.nn.logsumexp(score_prev, axis=0)
        diagonal = jnp.sum(score_own * identity, axis=1)
        return score_own, score_prev, row_lse, own_part, prev_part, diagonal

    score_own, score_prev, row_lse, own_part, prev_part, diagonal = lax.map(
        statistics, (image_blocks, text_blocks, prev_blocks))
    col_lse = jnp.logaddexp(own_part, jnp.roll(prev_part, -1, axis=0))
    pair_loss = (0.5 * (row_lse + col_lse) - diagonal).reshape(PAIRS)
    col_before = jnp.roll(col_lse, 1, axis=0)

    def gradients(block):
        left_rows, own_text, prev_text, tile_own, tile_prev, row_stat, col_here, col_prior = block
        prob_own = (0.5 * (jnp.exp(tile_own - row_stat[:, None]) + jnp.exp(tile_own - col_here[None, :]))
                    - identity).astype(jnp.bfloat16)
        prob_prev = (0.5 * (jnp.exp(tile_prev - row_stat[:, None])
                            + jnp.exp(tile_prev - col_prior[None, :]))).astype(jnp.bfloat16)
        image_part = factor * (jnp.dot(prob_own, own_text, preferred_element_type=jnp.float32)
                               + jnp.dot(prob_prev, prev_text, preferred_element_type=jnp.float32))
        own_term = jnp.dot(prob_own.T, left_rows, preferred_element_type=jnp.float32)
        prev_term = jnp.dot(prob_prev.T, left_rows, preferred_element_type=jnp.float32)
        return image_part.astype(jnp.bfloat16), own_term, prev_term

    image_grad, own_term, prev_term = lax.map(
        gradients, (image_blocks, text_blocks, prev_blocks, score_own, score_prev, row_lse, col_lse, col_before))
    text_grad = (factor * (own_term + jnp.roll(prev_term, -1, axis=0))).astype(jnp.bfloat16)
    return image_grad.reshape(PAIRS, WIDTH), text_grad.reshape(PAIRS, WIDTH), pair_loss
```

```python
import functools

import jax
import jax.numpy as jnp
from jax import lax
from jax.experimental import pallas as pl
from jax.experimental.pallas import tpu as pltpu
from jax.sharding import PartitionSpec as P

MESH = pl.DeviceIdType.MESH
F32 = jnp.float32
BF16 = jnp.bfloat16

Y_T = 0
Y_I = 2
C_I = 6
C_T = 7
X_T = 9
C_P = 13
C_F = 15
S_R = 19
S_C = 22
P_C = 24
V_X = 26
G_Y = 30
T_Y = 34
N_COPIES = 38


def dot_nt(a, b):
    return lax.dot_general(a, b, (((1,), (1,)), ((), ())), preferred_element_type=F32)


def dot_tn(a, b):
    return lax.dot_general(a, b, (((0,), (0,)), ((), ())), preferred_element_type=F32)


def dot_nn(a, b):
    return lax.dot_general(a, b, (((1,), (0,)), ((), ())), preferred_element_type=F32)


def log_add(a, b):
    top = jnp.maximum(a, b)
    return top + jnp.log(jnp.exp(a - top) + jnp.exp(b - top))


def kernel(
    n_dp,
    factor_ref,
    image_ref,
    text_ref,
    image_out,
    text_out,
    loss_out,
    full,
    cat,
    tail,
    row_exp,
    col_exp,
    col_max,
    col_part,
    row_max,
    row_part,
    row_scale,
    diag,
    col_stat,
    col_lse,
    prob,
    visit_out,
    visit_in,
    part_out,
    part_in,
    text_send,
    send_sem,
    recv_sem,
    local_sem,
):
    d = lax.axis_index("dp")
    m = lax.axis_index("mp")
    core = lax.rem(m, 2)
    c_m = m + 1 - 2 * core
    y_m = lax.rem(m + 2, 4)
    z_m = lax.rem(c_m + 2, 4)
    nxt = lax.rem(d + 1, n_dp)
    prv = lax.rem(d + n_dp - 1, n_dp)
    to_c, to_y, to_z = (d, c_m), (d, y_m), (d, z_m)
    to_next, to_prev = (nxt, m), (prv, m)

    def rows(index):
        return pl.ds(pl.multiple_of(index * 256, 256), 256)

    def remote(src, dst, index, device):
        return pltpu.make_async_remote_copy(
            src_ref=src,
            dst_ref=dst,
            send_sem=send_sem.at[index],
            recv_sem=recv_sem.at[index],
            device_id=device,
            device_id_type=MESH,
        )

    own = pl.ds(0, 256)
    via = pl.ds(256, 256)
    locals_ = [
        pltpu.make_async_copy(image_ref, full.at[:, own], local_sem.at[0]),
        pltpu.make_async_copy(text_ref.at[rows(m)], cat.at[pl.ds(512, 256), own], local_sem.at[1]),
        pltpu.make_async_copy(text_ref.at[rows(c_m)], cat.at[pl.ds(768, 256), own], local_sem.at[2]),
    ]
    for copy in locals_:
        copy.start()

    barrier = pltpu.get_barrier_semaphore()
    for device in (to_c, to_y, to_z, to_next, to_prev):
        pl.semaphore_signal(barrier, inc=1, device_id=device, device_id_type=MESH)
    pl.semaphore_wait(barrier, 5)

    y_text = [
        remote(text_ref.at[rows(y_m)], cat.at[pl.ds(512, 256), via], Y_T, to_y),
        remote(text_ref.at[rows(z_m)], cat.at[pl.ds(768, 256), via], Y_T + 1, to_y),
    ]

    def y_image(r):
        return remote(image_ref.at[rows(r)], full.at[rows(r), via], Y_I + r, to_y)

    c_image = remote(image_ref, full.at[:, pl.ds(512, 256)], C_I, to_c)
    c_text = [
        remote(text_ref.at[rows(c_m)], tail.at[1, :, own], C_T, to_c),
        remote(cat.at[pl.ds(768, 256), via], tail.at[1, :, via], C_T + 1, to_c),
    ]
    x_text = [
        remote(text_ref.at[rows(c_m)], cat.at[via, own], X_T, to_next),
        remote(text_ref.at[rows(m)], cat.at[own, own], X_T + 1, to_next),
        remote(cat.at[pl.ds(768, 256), via], cat.at[via, via], X_T + 2, to_next),
        remote(cat.at[pl.ds(512, 256), via], cat.at[own, via], X_T + 3, to_next),
    ]
    c_prev = [
        remote(cat.at[via, own], tail.at[0, :, own], C_P, to_c),
        remote(cat.at[via, via], tail.at[0, :, via], C_P + 1, to_c),
    ]

    def c_forward(r):
        return remote(full.at[rows(r), via], full.at[rows(r), pl.ds(768, 256)], C_F + r, to_c)

    y_text[1].start()
    y_text[0].start()
    x_text[0].start()
    x_text[1].start()
    c_text[0].start()
    c_image.start()
    for r in range(4):
        y_image(r).start()

    y_text[1].wait_recv()
    x_text[2].start()
    c_text[1].start()
    y_text[0].wait_recv()
    x_text[3].start()
    x_text[0].wait_recv()
    c_prev[0].start()
    x_text[2].wait_recv()
    c_prev[1].start()
    for copy in locals_:
        copy.wait()
    c_image.wait_recv()
    c_text[0].wait_recv()
    c_text[1].wait_recv()
    x_text[1].wait_recv()
    x_text[3].wait_recv()
    c_prev[0].wait_recv()
    c_prev[1].wait_recv()

    factor = factor_ref[0]
    eye = lax.broadcasted_iota(jnp.int32, (256, 256), 0) == lax.broadcasted_iota(
        jnp.int32, (256, 256), 1
    )

    def scores(r, carry):
        y_image(r).wait_recv()
        c_forward(r).start()
        c_forward(r).wait_recv()
        left = full[rows(r), 0:512]
        right = full[rows(r), 512:1024]
        prev = factor * (dot_nt(cat[0:256, :], left) + dot_nt(tail[0], right))
        mine = factor * (dot_nt(cat[512:768, :], left) + dot_nt(tail[1], right))
        top = jnp.maximum(
            jnp.max(prev, axis=0, keepdims=True), jnp.max(mine, axis=0, keepdims=True)
        )
        prev_exp = jnp.exp(prev - top)
        mine_exp = jnp.exp(mine - top)
        row_exp[r, 0:256, :] = prev_exp
        row_exp[r, 256:512, :] = mine_exp
        part = top + jnp.log(
            jnp.sum(prev_exp, axis=0, keepdims=True) + jnp.sum(mine_exp, axis=0, keepdims=True)
        )
        for k in range(2):
            lanes = slice(128 * k, 128 * k + 128)
            row_max[pl.ds(2 * r + k, 1), :] = top[:, lanes]
            row_part[0, pl.ds(2 * r + k, 1), :] = part[:, lanes]
        for tile, scored in enumerate((prev, mine)):
            highest = jnp.max(scored, axis=1, keepdims=True)
            scaled = jnp.exp(scored - highest)
            col_exp[r, 256 * tile : 256 * tile + 256, :] = scaled
            col_max[r, 256 * tile : 256 * tile + 256, :] = jnp.broadcast_to(highest, (256, 128))
            total = highest + jnp.log(jnp.sum(scaled, axis=1, keepdims=True))
            for k in range(2):
                piece = jnp.broadcast_to(total[128 * k : 128 * k + 128], (128, 128))
                col_part[r, 2 * tile + k : 2 * tile + k + 1, :] = piece.T[0:1, :]

        @pl.when(r == m)
        def _():
            found = jnp.sum(jnp.where(eye, mine, 0.0), axis=0, keepdims=True)
            for k in range(2):
                diag[k : k + 1, :] = found[:, 128 * k : 128 * k + 128]

        return carry

    lax.fori_loop(0, 4, scores, 0)

    highest = jnp.maximum(
        jnp.maximum(col_part[0, 0:4], col_part[1, 0:4]), jnp.maximum(col_part[2, 0:4], col_part[3, 0:4])
    )
    summed = (
        jnp.exp(col_part[0, 0:4] - highest)
        + jnp.exp(col_part[1, 0:4] - highest)
        + jnp.exp(col_part[2, 0:4] - highest)
        + jnp.exp(col_part[3, 0:4] - highest)
    )
    col_stat[0, 0:4, :] = highest + jnp.log(summed)
    col_stat[0, 4:8, :] = jnp.zeros((4, 128), F32)
    stats = [
        remote(col_stat.at[0], col_stat.at[1], S_C, to_prev),
        remote(col_stat.at[0], col_stat.at[2], S_C + 1, to_next),
        remote(row_part.at[0], row_part.at[1], S_R, to_y),
        remote(row_part.at[0], row_part.at[2], S_R + 1, to_c),
        remote(row_part.at[0], row_part.at[3], S_R + 2, to_z),
    ]
    for copy in stats:
        copy.start()
    for copy in stats:
        copy.wait_recv()

    parts = [row_part[k] for k in range(4)]
    highest = jnp.maximum(jnp.maximum(parts[0], parts[1]), jnp.maximum(parts[2], parts[3]))
    row_lse = highest + jnp.log(
        jnp.exp(parts[0] - highest)
        + jnp.exp(parts[1] - highest)
        + jnp.exp(parts[2] - highest)
        + jnp.exp(parts[3] - highest)
    )
    row_scale[...] = 0.5 * jnp.exp(row_max[...] - row_lse)
    lse_prev = log_add(col_stat[0, 0:2, :], col_stat[2, 2:4, :])
    lse_own = log_add(col_stat[0, 2:4, :], col_stat[1, 0:2, :])
    row_max[...] = row_lse
    loss_out[...] = 0.5 * (row_max[pl.ds(2 * m, 2), :] + lse_own) - diag[...]
    for tile, lse in enumerate((lse_prev, lse_own)):
        for k in range(2):
            at = 256 * tile + 128 * k
            col_lse[at : at + 128, :] = jnp.broadcast_to(lse[k : k + 1, :], (128, 128)).T

    p_copies = [
        remote(prob.at[pl.ds(512 * tile, 256)], prob.at[pl.ds(512 * tile + 256, 256)], P_C + tile, to_c)
        for tile in range(2)
    ]
    for tile in range(2):
        at = slice(256 * tile, 256 * tile + 256)
        for r in range(4):
            scale = 0.5 * jnp.exp(col_max[r, at, :] - col_lse[at, :])
            for k in range(2):
                lanes = slice(128 * k, 128 * k + 128)
                value = (
                    row_exp[r, at, lanes] * row_scale[2 * r + k : 2 * r + k + 1, :]
                    + col_exp[r, at, lanes] * scale
                )
                if tile == 1:
                    value = value - jnp.where(eye[:, lanes] & (m == r), 1.0, 0.0)
                prob[512 * tile : 512 * tile + 256, 256 * r + 128 * k : 256 * r + 128 * k + 128] = (
                    value.astype(BF16)
                )
        p_copies[tile].start()

    def visit(k):
        at = pl.ds(128 * k, 128)
        return remote(visit_out.at[at], visit_in.at[at], V_X + k, to_prev)

    def send_visit(k):
        visit_out[128 * k : 128 * k + 128, :] = dot_nn(
            prob[128 * k : 128 * k + 128, :], full[:, 0:512]
        ).astype(BF16)
        visit(k).start()

    def partial(r):
        return remote(part_out.at[rows(r)], part_in.at[rows(r)], G_Y + r, to_y)

    send_visit(0)
    send_visit(1)
    p_copies[0].wait_recv()
    p_copies[1].wait_recv()
    for r in range(4):
        part_out[256 * r : 256 * r + 256, :] = dot_tn(
            prob[:, 256 * r : 256 * r + 256], cat[:, 256:512]
        ).astype(BF16)
        partial(r).start()
        if r == 0:
            send_visit(2)
            send_visit(3)

    def text_final(k):
        target = rows(m) if k < 2 else rows(c_m)
        return remote(
            text_send.at[pl.ds(128 * k, 128)],
            text_out.at[target].at[pl.ds(128 * (k % 2), 128)],
            T_Y + k,
            to_y,
        )

    for k in range(4):
        own_term = dot_nn(prob[512 + 128 * k : 640 + 128 * k, :], full[:, 0:512])
        visit(k).wait_recv()
        value = factor * (own_term + visit_in[128 * k : 128 * k + 128, :].astype(F32))
        text_send[128 * k : 128 * k + 128, :] = value[:, 256:512].astype(BF16)
        text_final(k).start()
        start = (m if k < 2 else c_m) * 256 + 128 * (k % 2)
        text_out[pl.ds(pl.multiple_of(start, 128), 128), :] = value[:, 0:256].astype(BF16)

    for r in range(4):
        value = dot_tn(prob[:, 256 * r : 256 * r + 256], cat[:, 0:256])
        partial(r).wait_recv()
        image_out[256 * r : 256 * r + 256, :] = (
            factor * (value + part_in[256 * r : 256 * r + 256, :].astype(F32))
        ).astype(BF16)

    for k in range(4):
        text_final(k).wait_recv()
    for copy in y_text + c_text + x_text + c_prev + [c_image] + stats + p_copies:
        copy.wait_send()
    for r in range(4):
        y_image(r).wait_send()
        c_forward(r).wait_send()
        visit(r).wait_send()
        partial(r).wait_send()
        text_final(r).wait_send()


def local(n_dp, image_emb, text_emb, logit_scale):
    vmem = pltpu.VMEM
    image_grad, text_grad, loss = pl.pallas_call(
        functools.partial(kernel, n_dp),
        out_shape=(
            jax.ShapeDtypeStruct((1024, 256), BF16),
            jax.ShapeDtypeStruct((1024, 256), BF16),
            jax.ShapeDtypeStruct((2, 128), F32),
        ),
        in_specs=[
            pl.BlockSpec(memory_space=pltpu.SMEM),
            pl.BlockSpec(memory_space=pl.ANY),
            pl.BlockSpec(memory_space=pl.ANY),
        ],
        out_specs=[pl.BlockSpec(memory_space=vmem)] * 3,
        scratch_shapes=[
            vmem((1024, 1024), BF16),
            vmem((1024, 512), BF16),
            vmem((2, 256, 512), BF16),
            vmem((4, 512, 256), F32),
            vmem((4, 512, 256), F32),
            vmem((4, 512, 128), F32),
            vmem((4, 8, 128), F32),
            vmem((8, 128), F32),
            vmem((4, 8, 128), F32),
            vmem((8, 128), F32),
            vmem((2, 128), F32),
            vmem((3, 8, 128), F32),
            vmem((512, 128), F32),
            vmem((1024, 1024), BF16),
            vmem((512, 512), BF16),
            vmem((512, 512), BF16),
            vmem((1024, 256), BF16),
            vmem((1024, 256), BF16),
            vmem((512, 256), BF16),
            pltpu.SemaphoreType.DMA((N_COPIES,)),
            pltpu.SemaphoreType.DMA((N_COPIES,)),
            pltpu.SemaphoreType.DMA((3,)),
        ],
        compiler_params=pltpu.CompilerParams(
            collective_id=0, has_side_effects=True, vmem_limit_bytes=48 * 1024 * 1024
        ),
        cost_estimate=pl.CostEstimate(
            flops=3 * 2**31, bytes_accessed=2**21, transcendentals=2**20
        ),
    )(logit_scale, image_emb, text_emb)
    return image_grad, text_grad, loss.reshape(256)


def solution(mesh):
    return jax.shard_map(
        functools.partial(local, mesh.shape["dp"]),
        mesh=mesh,
        in_specs=(P("dp", "mp"), P("dp", "mp"), P()),
        out_specs=(P("dp", "mp"), P("dp", "mp"), P(("dp", "mp"))),
        check_vma=False,
    )
```

```python
import functools

import jax
import jax.numpy as jnp
from jax import lax
from jax.experimental import pallas as pl
from jax.experimental.pallas import tpu as pltpu
from jax.sharding import PartitionSpec as P

MESH = pl.DeviceIdType.MESH
F32 = jnp.float32
BF16 = jnp.bfloat16
CHUNKS = 8
PAIRS = 4

Y_T = 0
Y_I = 4
C_I = 12
C_T = 13
C_V = 15
X_T = 19
X_V = 23
C_P = 27
C_F = 31
S_R = 39
S_N = 40
S_P = 41
V_X = 42
G_Y = 46
T_Y = 54
L_Y = 58
N_COPIES = 59


def dot_nt(a, b):
    return lax.dot_general(a, b, (((1,), (1,)), ((), ())), preferred_element_type=F32)


def dot_tn(a, b):
    return lax.dot_general(a, b, (((0,), (0,)), ((), ())), preferred_element_type=F32)


def dot_nn(a, b):
    return lax.dot_general(a, b, (((1,), (0,)), ((), ())), preferred_element_type=F32)


def log_add(a, b):
    top = jnp.maximum(a, b)
    return top + jnp.log(jnp.exp(a - top) + jnp.exp(b - top))


def kernel(
    n_dp,
    factor_ref,
    image_ref,
    text_ref,
    image_out,
    text_out,
    loss_out,
    full,
    text,
    score,
    row_part,
    col_max,
    col_sum,
    stat,
    row_lse,
    col_lse,
    prob,
    visit_out,
    visit_in,
    part_out,
    part_in,
    text_send,
    text_keep,
    image_keep,
    loss_own,
    loss_in,
    send_sem,
    recv_sem,
    local_sem,
):
    d = lax.axis_index("dp")
    m = lax.axis_index("mp")
    c_m = m + 1 - 2 * lax.rem(m, 2)
    y_m = lax.rem(m + 2, 4)
    nxt = lax.rem(d + 1, n_dp)
    prv = lax.rem(d + n_dp - 1, n_dp)
    half = n_dp // 2
    swap = lax.div(d, half)
    out_swap = lax.div(lax.rem(d, half) + 1, half)
    back_swap = 1 - lax.div(lax.rem(d, half) + half - 1, half)
    to_c, to_y = (d, c_m), (d, y_m)
    to_next = (nxt, lax.rem(m + 2 * out_swap, 4))
    to_prev = (prv, lax.rem(m + 2 * back_swap, 4))
    mine = lax.rem(m + 2 * swap, 4)
    other = lax.rem(c_m + 2 * swap, 4)
    mine_y = lax.rem(mine + 2, 4)
    other_y = lax.rem(other + 2, 4)

    def block(index, size=256):
        return pl.ds(pl.multiple_of(index * size, size), size)

    def remote(src, dst, index, device):
        return pltpu.make_async_remote_copy(
            src_ref=src,
            dst_ref=dst,
            send_sem=send_sem.at[index],
            recv_sem=recv_sem.at[index],
            device_id=device,
            device_id_type=MESH,
        )

    own, via = pl.ds(0, 256), pl.ds(256, 256)

    def piece(first, second, k):
        return block(2 * (first if k < 2 else second) + k % 2, 128)

    locals_ = [
        pltpu.make_async_copy(image_ref, full.at[:, own], local_sem.at[0]),
        pltpu.make_async_copy(text_ref.at[block(mine)], text.at[pl.ds(512, 256), own], local_sem.at[1]),
        pltpu.make_async_copy(text_ref.at[block(other)], text.at[pl.ds(768, 256), own], local_sem.at[2]),
    ]
    for copy in locals_:
        copy.start()

    barrier = pltpu.get_barrier_semaphore()
    for device in (to_c, to_y, to_prev):
        pl.semaphore_signal(barrier, inc=1, device_id=device, device_id_type=MESH)
    pl.semaphore_wait(barrier, 3)

    y_text = [
        remote(text_ref.at[piece(mine_y, other_y, k)], text.at[pl.ds(512 + 128 * k, 128), via], Y_T + k, to_y)
        for k in range(4)
    ]
    c_image = remote(image_ref, full.at[:, pl.ds(512, 256)], C_I, to_c)
    c_text = [
        remote(text_ref.at[block(other)], text.at[pl.ds(512, 256), pl.ds(512, 256)], C_T, to_c),
        remote(text_ref.at[block(mine)], text.at[pl.ds(768, 256), pl.ds(512, 256)], C_T + 1, to_c),
    ]
    c_via = [
        remote(
            text.at[pl.ds(512 + 128 * k, 128), via],
            text.at[pl.ds(512 + 128 * ((k + 2) % 4), 128), pl.ds(768, 256)],
            C_V + k,
            to_c,
        )
        for k in range(4)
    ]
    x_own = [
        remote(text_ref.at[piece(mine, other, k)], text.at[pl.ds(128 * k, 128), block(out_swap)], X_T + k, to_next)
        for k in range(4)
    ]
    x_via = [
        remote(
            text.at[pl.ds(512 + 128 * k, 128), via],
            text.at[pl.ds(128 * k, 128), block(1 - out_swap)],
            X_V + k,
            to_next,
        )
        for k in range(4)
    ]
    c_prev = [
        remote(
            text.at[pl.ds(128 * k, 128), pl.ds(0, 512)],
            text.at[pl.ds(128 * ((k + 2) % 4), 128), pl.ds(512, 512)],
            C_P + k,
            to_c,
        )
        for k in range(4)
    ]

    def y_image(r):
        return remote(image_ref.at[block(r, 128)], full.at[block(r, 128), via], Y_I + r, to_y)

    def c_forward(r):
        return remote(full.at[block(r, 128), via], full.at[block(r, 128), pl.ds(768, 256)], C_F + r, to_c)

    for k in range(4):
        y_text[k].start()
    for k in range(4):
        x_own[k].start()
    c_text[0].start()
    c_text[1].start()
    c_image.start()
    for r in range(CHUNKS):
        y_image(r).start()

    for k in range(4):
        y_text[k].wait_recv()
        x_via[k].start()
        c_via[k].start()
    for copy in locals_:
        copy.wait()
    for copy in [c_image] + c_text + c_via:
        copy.wait_recv()
    sent = y_text + [c_image] + c_text + c_via + x_own + x_via + c_prev

    factor = factor_ref[0]
    eye = lax.broadcasted_iota(jnp.int32, (128, 128), 0) == lax.broadcasted_iota(
        jnp.int32, (128, 128), 1
    )

    def arrive(p):
        for r in (2 * p, 2 * p + 1):
            y_image(r).wait_recv()
            c_forward(r).start()
        for r in (2 * p, 2 * p + 1):
            c_forward(r).wait_recv()

    def tile(t, p):
        scored = factor * dot_nt(text[512 * t : 512 * t + 512, :], full[block(p), :])
        score[p, 512 * t : 512 * t + 512, :] = scored
        top = jnp.max(scored, axis=0, keepdims=True)
        total = top + jnp.log(jnp.sum(jnp.exp(scored - top), axis=0, keepdims=True))
        for k in range(2):
            row_part[t, pl.ds(2 * p + k, 1), :] = total[:, 128 * k : 128 * k + 128]
        highest = jnp.max(scored, axis=1, keepdims=True)
        summed = jnp.sum(jnp.exp(scored - highest), axis=1, keepdims=True)
        for q in range(4):
            at = slice(128 * q, 128 * q + 128)
            col_max[p, 4 * t + q : 4 * t + q + 1, :] = jnp.sum(
                jnp.where(eye, highest[at], 0.0), axis=0, keepdims=True
            )
            col_sum[p, 4 * t + q : 4 * t + q + 1, :] = jnp.sum(
                jnp.where(eye, summed[at], 0.0), axis=0, keepdims=True
            )

    def own_chunk(p, carry):
        arrive(p)
        tile(1, p)
        return carry

    def prev_chunk(p, carry):
        tile(0, p)
        return carry

    def column(t):
        rows = slice(4 * t, 4 * t + 4)
        top = col_max[0, rows, :]
        for p in range(1, PAIRS):
            top = jnp.maximum(top, col_max[p, rows, :])
        total = jnp.zeros_like(top)
        for p in range(PAIRS):
            total = total + col_sum[p, rows, :] * jnp.exp(col_max[p, rows, :] - top)
        at = 2 - 2 * t
        stat[at, 0:4, :] = top + jnp.log(total)
        stat[at, 4:8, :] = jnp.zeros((4, 128), F32)

    to_n = remote(stat.at[0], stat.at[3], S_N, to_next)
    to_p = remote(stat.at[2], stat.at[1], S_P, to_prev)
    to_r = remote(stat.at[4], stat.at[5], S_R, to_y)

    first = lax.rem(d, half) == 0
    early = jnp.where(first, PAIRS, 2)
    later = jnp.where(first, PAIRS, 3)
    lax.fori_loop(0, early, own_chunk, 0)

    @pl.when(first)
    def _():
        column(1)
        to_n.start()

    for k in range(4):
        x_own[k].wait_recv()
        x_via[k].wait_recv()
        c_prev[k].start()
    for k in range(4):
        c_prev[k].wait_recv()
    lax.fori_loop(0, early, prev_chunk, 0)
    lax.fori_loop(early, later, own_chunk, 0)
    lax.fori_loop(early, later, prev_chunk, 0)
    lax.fori_loop(later, PAIRS, own_chunk, 0)

    @pl.when(jnp.logical_not(first))
    def _():
        column(1)
        to_n.start()

    lax.fori_loop(later, PAIRS, prev_chunk, 0)
    stat[4] = log_add(row_part[0], row_part[1])
    to_r.start()
    column(0)
    to_p.start()
    sent += [to_n, to_p, to_r]

    place = [2 * mine, 2 * mine + 1, 2 * other, 2 * other + 1]

    def diagonal_block(q):
        pair = mine if q < 2 else other
        return score[pair, 512 + 128 * q : 640 + 128 * q, 128 * (q % 2) : 128 * (q % 2) + 128]

    diagonal = [
        jnp.sum(
            jnp.where(eye, diagonal_block(q), 0.0), axis=0, keepdims=True
        )
        for q in range(4)
    ]

    def spread(lse, at):
        for q in range(4):
            col_lse[at + 128 * q : at + 128 * q + 128, :] = jnp.broadcast_to(
                lse[q : q + 1, :], (128, 128)
            ).T

    to_p.wait_recv()
    lse_own = log_add(stat[0, 0:4, :], stat[1, 0:4, :])
    spread(lse_own, 512)
    to_r.wait_recv()
    row_lse[...] = log_add(stat[4], stat[5])
    for q in range(4):
        loss_own[q : q + 1, :] = (
            0.5 * (row_lse[pl.ds(place[q], 1), :] + lse_own[q : q + 1, :]) - diagonal[q]
        )
    loss_own[4:8, :] = jnp.zeros((4, 128), F32)
    loss_copy = remote(loss_own, loss_in, L_Y, to_y)
    to_n.wait_recv()
    spread(log_add(stat[2, 0:4, :], stat[3, 0:4, :]), 0)

    def partial(r):
        return remote(part_out.at[block(r, 128)], part_in.at[block(r, 128)], G_Y + r, to_y)

    unit = eye.astype(F32)

    def probability(p, carry):
        for k in range(2):
            r = 2 * p + k
            lanes = block(r, 128)
            row = row_lse[pl.ds(r, 1), :]
            for q in range(8):
                at = slice(128 * q, 128 * q + 128)
                scored = score[p, at, 128 * k : 128 * k + 128]
                value = 0.5 * (jnp.exp(scored - row) + jnp.exp(scored - col_lse[at, :]))
                if q >= 4:
                    value = value - jnp.where(r == place[q - 4], unit, 0.0)
                prob[at, lanes] = value.astype(BF16)
            part_out[lanes, :] = dot_tn(prob[:, lanes], text[:, 256:512]).astype(BF16)
            partial(r).start()
        return carry

    lax.fori_loop(0, PAIRS, probability, 0)
    loss_copy.start()

    def visit(k):
        rows = pl.ds(256 * (k % 2), 256)
        kept = 1 - k // 2
        taken = lax.rem(kept + back_swap, 2)
        return remote(
            visit_out.at[rows, block(taken)], visit_in.at[rows, pl.ds(256 * kept, 256)], V_X + k, to_prev
        )

    for kept in (1, 0):
        lanes = block(lax.rem(kept + back_swap, 2))
        for rows in (slice(0, 256), slice(256, 512)):
            visit_out[rows, lanes] = dot_nn(prob[rows, :], full[:, lanes]).astype(BF16)
        visit(2 * (1 - kept)).start()
        visit(2 * (1 - kept) + 1).start()

    image_copies = [
        pltpu.make_async_copy(
            image_keep.at[pl.ds(512 * k, 512)], image_out.at[pl.ds(512 * k, 512)], local_sem.at[3 + k]
        )
        for k in range(2)
    ]

    def image_final(r, carry):
        lanes = block(r, 128)
        value = dot_tn(prob[:, lanes], text[:, 0:256])
        partial(r).wait_recv()
        image_keep[lanes, :] = (factor * (value + part_in[lanes, :].astype(F32))).astype(BF16)
        return carry

    def text_value(k):
        rows = slice(256 * (k % 2), 256 * (k % 2) + 256)
        lanes = slice(256, 512) if k < 2 else slice(0, 256)
        own_term = dot_nn(prob[512 + rows.start : 512 + rows.stop, :], full[:, lanes])
        visit(k).wait_recv()
        return (factor * (own_term + visit_in[rows, lanes].astype(F32))).astype(BF16)

    text_copies = []
    for k in range(2):
        rows = pl.ds(256 * k, 256)
        target = text_out.at[block(mine if k == 0 else other)]
        text_copies.append(remote(text_send.at[rows], target, T_Y + k, to_y))
    keep_copies = [
        pltpu.make_async_copy(
            text_keep.at[pl.ds(256 * k, 256)],
            text_out.at[block(mine if k == 0 else other)],
            local_sem.at[5 + k],
        )
        for k in range(2)
    ]

    lax.fori_loop(0, 4, image_final, 0)
    image_copies[0].start()
    for k in range(2):
        text_send[256 * k : 256 * k + 256, :] = text_value(k)
        text_copies[k].start()
    lax.fori_loop(4, CHUNKS, image_final, 0)
    image_copies[1].start()
    for k in range(2):
        text_keep[256 * k : 256 * k + 256, :] = text_value(2 + k)
        keep_copies[k].start()

    loss_copy.wait_recv()
    loss_out[...] = jnp.where(swap == 1, loss_in[0:2, :], loss_own[0:2, :])
    for copy in sent + [loss_copy] + text_copies:
        copy.wait_send()
    for k in range(4):
        visit(k).wait_send()
    for r in range(CHUNKS):
        y_image(r).wait_send()
        c_forward(r).wait_send()
        partial(r).wait_send()
    for copy in image_copies + keep_copies:
        copy.wait()
    for copy in text_copies:
        copy.wait_recv()


def local(n_dp, image_emb, text_emb, logit_scale):
    vmem = pltpu.VMEM
    image_grad, text_grad, loss = pl.pallas_call(
        functools.partial(kernel, n_dp),
        out_shape=(
            jax.ShapeDtypeStruct((1024, 256), BF16),
            jax.ShapeDtypeStruct((1024, 256), BF16),
            jax.ShapeDtypeStruct((2, 128), F32),
        ),
        in_specs=[
            pl.BlockSpec(memory_space=pltpu.SMEM),
            pl.BlockSpec(memory_space=pl.ANY),
            pl.BlockSpec(memory_space=pl.ANY),
        ],
        out_specs=[
            pl.BlockSpec(memory_space=pl.ANY),
            pl.BlockSpec(memory_space=pl.ANY),
            pl.BlockSpec(memory_space=vmem),
        ],
        scratch_shapes=[
            vmem((1024, 1024), BF16),
            vmem((1024, 1024), BF16),
            vmem((PAIRS, 1024, 256), F32),
            vmem((2, 8, 128), F32),
            vmem((PAIRS, 8, 128), F32),
            vmem((PAIRS, 8, 128), F32),
            vmem((6, 8, 128), F32),
            vmem((8, 128), F32),
            vmem((1024, 128), F32),
            vmem((1024, 1024), BF16),
            vmem((512, 512), BF16),
            vmem((512, 512), BF16),
            vmem((1024, 256), BF16),
            vmem((1024, 256), BF16),
            vmem((512, 256), BF16),
            vmem((512, 256), BF16),
            vmem((1024, 256), BF16),
            vmem((8, 128), F32),
            vmem((8, 128), F32),
            pltpu.SemaphoreType.DMA((N_COPIES,)),
            pltpu.SemaphoreType.DMA((N_COPIES,)),
            pltpu.SemaphoreType.DMA((7,)),
        ],
        compiler_params=pltpu.CompilerParams(
            collective_id=0, has_side_effects=True, vmem_limit_bytes=60 * 1024 * 1024
        ),
        cost_estimate=pl.CostEstimate(
            flops=4 * 2**31, bytes_accessed=2**21, transcendentals=2**22
        ),
    )(logit_scale, image_emb, text_emb)
    return image_grad, text_grad, loss.reshape(256)


def solution(mesh):
    return jax.shard_map(
        functools.partial(local, mesh.shape["dp"]),
        mesh=mesh,
        in_specs=(P("dp", "mp"), P("dp", "mp"), P()),
        out_specs=(P("dp", "mp"), P("dp", "mp"), P(("dp", "mp"))),
        check_vma=False,
    )
```

```python
import functools

import jax
import jax.numpy as jnp
from jax import lax
from jax.experimental import pallas as pl
from jax.experimental.pallas import tpu as pltpu
from jax.sharding import PartitionSpec as P

MESH = pl.DeviceIdType.MESH
F32 = jnp.float32
BF16 = jnp.bfloat16
CHUNKS = 8
PAIRS = 4

Y_T = 0
Y_I = 4
C_I = 12
C_T = 13
C_V = 15
X_T = 19
X_V = 23
C_P = 27
C_F = 31
S_R = 39
S_N = 40
S_P = 41
V_X = 42
G_Y = 46
T_Y = 54
L_Y = 58
N_COPIES = 59


def dot_nt(a, b):
    return lax.dot_general(a, b, (((1,), (1,)), ((), ())), preferred_element_type=F32)


def dot_tn(a, b):
    return lax.dot_general(a, b, (((0,), (0,)), ((), ())), preferred_element_type=F32)


def dot_nn(a, b):
    return lax.dot_general(a, b, (((1,), (0,)), ((), ())), preferred_element_type=F32)


def log_add(a, b):
    top = jnp.maximum(a, b)
    return top + jnp.log(jnp.exp(a - top) + jnp.exp(b - top))


def kernel(
    n_dp,
    factor_ref,
    image_ref,
    text_ref,
    image_out,
    text_out,
    loss_out,
    full,
    text,
    score,
    row_part,
    col_max,
    col_sum,
    stat,
    row_lse,
    col_lse,
    prob,
    visit_out,
    visit_in,
    part_out,
    part_in,
    text_send,
    loss_own,
    loss_in,
    send_sem,
    recv_sem,
    local_sem,
):
    d = lax.axis_index("dp")
    m = lax.axis_index("mp")
    c_m = m + 1 - 2 * lax.rem(m, 2)
    y_m = lax.rem(m + 2, 4)
    nxt = lax.rem(d + 1, n_dp)
    prv = lax.rem(d + n_dp - 1, n_dp)
    half = n_dp // 2
    swap = lax.div(d, half)
    out_swap = lax.div(lax.rem(d, half) + 1, half)
    back_swap = 1 - lax.div(lax.rem(d, half) + half - 1, half)
    to_c, to_y = (d, c_m), (d, y_m)
    to_next = (nxt, lax.rem(m + 2 * out_swap, 4))
    to_prev = (prv, lax.rem(m + 2 * back_swap, 4))
    mine = lax.rem(m + 2 * swap, 4)
    other = lax.rem(c_m + 2 * swap, 4)
    mine_y = lax.rem(mine + 2, 4)
    other_y = lax.rem(other + 2, 4)

    def block(index, size=256):
        return pl.ds(pl.multiple_of(index * size, size), size)

    def remote(src, dst, index, device):
        return pltpu.make_async_remote_copy(
            src_ref=src,
            dst_ref=dst,
            send_sem=send_sem.at[index],
            recv_sem=recv_sem.at[index],
            device_id=device,
            device_id_type=MESH,
        )

    own, via = pl.ds(0, 256), pl.ds(256, 256)

    def piece(first, second, k):
        return block(2 * (first if k < 2 else second) + k % 2, 128)

    locals_ = [
        pltpu.make_async_copy(image_ref, full.at[:, own], local_sem.at[0]),
        pltpu.make_async_copy(text_ref.at[block(mine)], text.at[pl.ds(512, 256), own], local_sem.at[1]),
        pltpu.make_async_copy(text_ref.at[block(other)], text.at[pl.ds(768, 256), own], local_sem.at[2]),
    ]
    for copy in locals_:
        copy.start()

    barrier = pltpu.get_barrier_semaphore()
    for device in (to_c, to_y, to_prev):
        pl.semaphore_signal(barrier, inc=1, device_id=device, device_id_type=MESH)
    pl.semaphore_wait(barrier, 3)

    y_text = [
        remote(text_ref.at[piece(mine_y, other_y, k)], text.at[pl.ds(512 + 128 * k, 128), via], Y_T + k, to_y)
        for k in range(4)
    ]
    c_image = remote(image_ref, full.at[:, pl.ds(512, 256)], C_I, to_c)
    c_text = [
        remote(text_ref.at[block(other)], text.at[pl.ds(512, 256), pl.ds(512, 256)], C_T, to_c),
        remote(text_ref.at[block(mine)], text.at[pl.ds(768, 256), pl.ds(512, 256)], C_T + 1, to_c),
    ]
    c_via = [
        remote(
            text.at[pl.ds(512 + 128 * k, 128), via],
            text.at[pl.ds(512 + 128 * ((k + 2) % 4), 128), pl.ds(768, 256)],
            C_V + k,
            to_c,
        )
        for k in range(4)
    ]
    x_own = [
        remote(text_ref.at[piece(mine, other, k)], text.at[pl.ds(128 * k, 128), block(out_swap)], X_T + k, to_next)
        for k in range(4)
    ]
    x_via = [
        remote(
            text.at[pl.ds(512 + 128 * k, 128), via],
            text.at[pl.ds(128 * k, 128), block(1 - out_swap)],
            X_V + k,
            to_next,
        )
        for k in range(4)
    ]
    c_prev = [
        remote(
            text.at[pl.ds(128 * k, 128), pl.ds(0, 512)],
            text.at[pl.ds(128 * ((k + 2) % 4), 128), pl.ds(512, 512)],
            C_P + k,
            to_c,
        )
        for k in range(4)
    ]

    def y_image(r):
        return remote(image_ref.at[block(r, 128)], full.at[block(r, 128), via], Y_I + r, to_y)

    def c_forward(r):
        return remote(full.at[block(r, 128), via], full.at[block(r, 128), pl.ds(768, 256)], C_F + r, to_c)

    for k in range(4):
        y_text[k].start()
    for k in range(4):
        x_own[k].start()
    c_text[0].start()
    c_text[1].start()
    c_image.start()
    for r in range(CHUNKS):
        y_image(r).start()

    for k in range(4):
        y_text[k].wait_recv()
        x_via[k].start()
        c_via[k].start()
    for copy in locals_:
        copy.wait()
    for copy in [c_image] + c_text + c_via:
        copy.wait_recv()
    sent = y_text + [c_image] + c_text + c_via + x_own + x_via + c_prev

    factor = factor_ref[0]
    eye = lax.broadcasted_iota(jnp.int32, (128, 128), 0) == lax.broadcasted_iota(
        jnp.int32, (128, 128), 1
    )

    def arrive(p):
        for r in (2 * p, 2 * p + 1):
            y_image(r).wait_recv()
            c_forward(r).start()
        for r in (2 * p, 2 * p + 1):
            c_forward(r).wait_recv()

    def tile(t, p):
        scored = factor * dot_nt(text[512 * t : 512 * t + 512, :], full[block(p), :])
        score[p, 512 * t : 512 * t + 512, :] = scored
        top = jnp.max(scored, axis=0, keepdims=True)
        total = top + jnp.log(jnp.sum(jnp.exp(scored - top), axis=0, keepdims=True))
        for k in range(2):
            row_part[t, pl.ds(2 * p + k, 1), :] = total[:, 128 * k : 128 * k + 128]
        highest = jnp.max(scored, axis=1, keepdims=True)
        summed = jnp.sum(jnp.exp(scored - highest), axis=1, keepdims=True)
        for q in range(4):
            at = slice(128 * q, 128 * q + 128)
            col_max[p, 4 * t + q : 4 * t + q + 1, :] = jnp.sum(
                jnp.where(eye, highest[at], 0.0), axis=0, keepdims=True
            )
            col_sum[p, 4 * t + q : 4 * t + q + 1, :] = jnp.sum(
                jnp.where(eye, summed[at], 0.0), axis=0, keepdims=True
            )

    def own_chunk(p, carry):
        arrive(p)
        tile(1, p)
        return carry

    def prev_chunk(p, carry):
        tile(0, p)
        return carry

    def column(t):
        rows = slice(4 * t, 4 * t + 4)
        top = col_max[0, rows, :]
        for p in range(1, PAIRS):
            top = jnp.maximum(top, col_max[p, rows, :])
        total = jnp.zeros_like(top)
        for p in range(PAIRS):
            total = total + col_sum[p, rows, :] * jnp.exp(col_max[p, rows, :] - top)
        at = 2 - 2 * t
        stat[at, 0:4, :] = top + jnp.log(total)
        stat[at, 4:8, :] = jnp.zeros((4, 128), F32)

    to_n = remote(stat.at[0], stat.at[3], S_N, to_next)
    to_p = remote(stat.at[2], stat.at[1], S_P, to_prev)
    to_r = remote(stat.at[4], stat.at[5], S_R, to_y)

    lax.fori_loop(0, PAIRS, own_chunk, 0)
    column(1)
    to_n.start()
    for k in range(4):
        x_own[k].wait_recv()
        x_via[k].wait_recv()
        c_prev[k].start()
    for k in range(4):
        c_prev[k].wait_recv()
    lax.fori_loop(0, PAIRS, prev_chunk, 0)
    stat[4] = log_add(row_part[0], row_part[1])
    to_r.start()
    column(0)
    to_p.start()
    sent += [to_n, to_p, to_r]

    place = [2 * mine, 2 * mine + 1, 2 * other, 2 * other + 1]

    def diagonal_block(q):
        pair = mine if q < 2 else other
        return score[pair, 512 + 128 * q : 640 + 128 * q, 128 * (q % 2) : 128 * (q % 2) + 128]

    diagonal = [
        jnp.sum(
            jnp.where(eye, diagonal_block(q), 0.0), axis=0, keepdims=True
        )
        for q in range(4)
    ]

    def spread(lse, at):
        for q in range(4):
            col_lse[at + 128 * q : at + 128 * q + 128, :] = jnp.broadcast_to(
                lse[q : q + 1, :], (128, 128)
            ).T

    to_p.wait_recv()
    lse_own = log_add(stat[0, 0:4, :], stat[1, 0:4, :])
    spread(lse_own, 512)
    to_r.wait_recv()
    row_lse[...] = log_add(stat[4], stat[5])
    for q in range(4):
        loss_own[q : q + 1, :] = (
            0.5 * (row_lse[pl.ds(place[q], 1), :] + lse_own[q : q + 1, :]) - diagonal[q]
        )
    loss_own[4:8, :] = jnp.zeros((4, 128), F32)
    loss_copy = remote(loss_own, loss_in, L_Y, to_y)
    unit = eye.astype(F32)

    def probability(p, k, q):
        at = slice(128 * q, 128 * q + 128)
        r = 2 * p + k
        scored = score[p, at, 128 * k : 128 * k + 128]
        row = row_lse[pl.ds(r, 1), :]
        value = 0.5 * (jnp.exp(scored - row) + jnp.exp(scored - col_lse[at, :]))
        if q >= 4:
            value = value - jnp.where(r == place[q - 4], unit, 0.0)
        prob[at, block(r, 128)] = value.astype(BF16)

    def own_probability(p, carry):
        for k in range(2):
            for q in range(4, 8):
                probability(p, k, q)
        return carry

    lax.fori_loop(0, PAIRS, own_probability, 0)
    to_n.wait_recv()
    spread(log_add(stat[2, 0:4, :], stat[3, 0:4, :]), 0)

    def partial(r):
        return remote(part_out.at[block(r, 128)], part_in.at[block(r, 128)], G_Y + r, to_y)

    def prev_probability(p, carry):
        for k in range(2):
            for q in range(4):
                probability(p, k, q)
            lanes = block(2 * p + k, 128)
            part_out[lanes, :] = dot_tn(prob[:, lanes], text[:, 256:512]).astype(BF16)
            partial(2 * p + k).start()
        return carry

    lax.fori_loop(0, PAIRS, prev_probability, 0)
    loss_copy.start()

    def visit(k):
        rows = pl.ds(256 * (k % 2), 256)
        kept = 1 - k // 2
        taken = lax.rem(kept + back_swap, 2)
        return remote(
            visit_out.at[rows, block(taken)], visit_in.at[rows, pl.ds(256 * kept, 256)], V_X + k, to_prev
        )

    for kept in (1, 0):
        lanes = block(lax.rem(kept + back_swap, 2))
        for rows in (slice(0, 256), slice(256, 512)):
            visit_out[rows, lanes] = dot_nn(prob[rows, :], full[:, lanes]).astype(BF16)
        visit(2 * (1 - kept)).start()
        visit(2 * (1 - kept) + 1).start()

    def image_final(r, carry):
        lanes = block(r, 128)
        value = dot_tn(prob[:, lanes], text[:, 0:256])
        partial(r).wait_recv()
        image_out[lanes, :] = (factor * (value + part_in[lanes, :].astype(F32))).astype(BF16)
        return carry

    def text_value(k):
        rows = slice(256 * (k % 2), 256 * (k % 2) + 256)
        lanes = slice(256, 512) if k < 2 else slice(0, 256)
        own_term = dot_nn(prob[512 + rows.start : 512 + rows.stop, :], full[:, lanes])
        visit(k).wait_recv()
        return (factor * (own_term + visit_in[rows, lanes].astype(F32))).astype(BF16)

    text_copies = []
    for k in range(2):
        rows = pl.ds(256 * k, 256)
        target = text_out.at[block(mine if k == 0 else other)]
        text_copies.append(remote(text_send.at[rows], target, T_Y + k, to_y))
    lax.fori_loop(0, 4, image_final, 0)
    for k in range(2):
        text_send[256 * k : 256 * k + 256, :] = text_value(k)
        text_copies[k].start()
    lax.fori_loop(4, CHUNKS, image_final, 0)
    for k in range(2):
        text_out[block(mine if k == 0 else other), :] = text_value(2 + k)

    loss_copy.wait_recv()
    loss_out[...] = jnp.where(swap == 1, loss_in[0:2, :], loss_own[0:2, :])
    for copy in sent + [loss_copy] + text_copies:
        copy.wait_send()
    for k in range(4):
        visit(k).wait_send()
    for r in range(CHUNKS):
        y_image(r).wait_send()
        c_forward(r).wait_send()
        partial(r).wait_send()
    for copy in text_copies:
        copy.wait_recv()


def finish(image_ref, text_ref, loss_ref, image_out, text_out, loss_out, sem):
    copies = [
        pltpu.make_async_copy(image_ref, image_out, sem.at[0]),
        pltpu.make_async_copy(text_ref, text_out, sem.at[1]),
    ]
    for copy in copies:
        copy.start()
    for k in range(2):
        loss_out[pl.ds(128 * k, 128)] = loss_ref[k, :]
    for copy in copies:
        copy.wait()


def local(n_dp, image_emb, text_emb, logit_scale):
    vmem = pltpu.VMEM
    image_grad, text_grad, loss = pl.pallas_call(
        functools.partial(kernel, n_dp),
        out_shape=(
            vmem((1024, 256), BF16),
            vmem((1024, 256), BF16),
            vmem((2, 128), F32),
        ),
        in_specs=[
            pl.BlockSpec(memory_space=pltpu.SMEM),
            pl.BlockSpec(memory_space=pl.ANY),
            pl.BlockSpec(memory_space=pl.ANY),
        ],
        out_specs=[pl.BlockSpec(memory_space=vmem)] * 3,
        scratch_shapes=[
            vmem((1024, 1024), BF16),
            vmem((1024, 1024), BF16),
            vmem((PAIRS, 1024, 256), F32),
            vmem((2, 8, 128), F32),
            vmem((PAIRS, 8, 128), F32),
            vmem((PAIRS, 8, 128), F32),
            vmem((6, 8, 128), F32),
            vmem((8, 128), F32),
            vmem((1024, 128), F32),
            vmem((1024, 1024), BF16),
            vmem((512, 512), BF16),
            vmem((512, 512), BF16),
            vmem((1024, 256), BF16),
            vmem((1024, 256), BF16),
            vmem((512, 256), BF16),
            vmem((8, 128), F32),
            vmem((8, 128), F32),
            pltpu.SemaphoreType.DMA((N_COPIES,)),
            pltpu.SemaphoreType.DMA((N_COPIES,)),
            pltpu.SemaphoreType.DMA((3,)),
        ],
        compiler_params=pltpu.CompilerParams(
            collective_id=0, has_side_effects=True, vmem_limit_bytes=56 * 1024 * 1024
        ),
        cost_estimate=pl.CostEstimate(
            flops=4 * 2**31, bytes_accessed=2**21, transcendentals=2**22
        ),
    )(logit_scale, image_emb, text_emb)
    return pl.pallas_call(
        finish,
        out_shape=(
            jax.ShapeDtypeStruct((1024, 256), BF16),
            jax.ShapeDtypeStruct((1024, 256), BF16),
            jax.ShapeDtypeStruct((256,), F32),
        ),
        in_specs=[pl.BlockSpec(memory_space=vmem)] * 3,
        out_specs=[
            pl.BlockSpec(memory_space=pl.ANY),
            pl.BlockSpec(memory_space=pl.ANY),
            pl.BlockSpec(memory_space=vmem),
        ],
        scratch_shapes=[pltpu.SemaphoreType.DMA((2,))],
    )(*(pltpu.with_memory_space_constraint(x, vmem) for x in (image_grad, text_grad, loss)))


def solution(mesh):
    return jax.shard_map(
        functools.partial(local, mesh.shape["dp"]),
        mesh=mesh,
        in_specs=(P("dp", "mp"), P("dp", "mp"), P()),
        out_specs=(P("dp", "mp"), P("dp", "mp"), P(("dp", "mp"))),
        check_vma=False,
    )
```

```python
import functools

import jax
import jax.numpy as jnp
from jax import lax
from jax.experimental import pallas as pl
from jax.experimental.pallas import tpu as pltpu
from jax.sharding import PartitionSpec as P

MESH = pl.DeviceIdType.MESH
F32 = jnp.float32
BF16 = jnp.bfloat16
CHUNKS = 8
PAIRS = 4

Y_T = 0
Y_I = 4
C_I = 12
C_T = 13
C_V = 15
X_T = 19
X_V = 23
C_P = 27
C_F = 31
S_R = 39
S_N = 40
S_P = 41
V_X = 42
G_Y = 46
T_Y = 54
L_Y = 58
R_A = 59
R_B = 60
N_COPIES = 61


def dot_nt(a, b):
    return lax.dot_general(a, b, (((1,), (1,)), ((), ())), preferred_element_type=F32)


def dot_tn(a, b):
    return lax.dot_general(a, b, (((0,), (0,)), ((), ())), preferred_element_type=F32)


def dot_nn(a, b):
    return lax.dot_general(a, b, (((1,), (0,)), ((), ())), preferred_element_type=F32)


def log_add(a, b):
    top = jnp.maximum(a, b)
    return top + jnp.log(jnp.exp(a - top) + jnp.exp(b - top))


def kernel(
    n_dp,
    factor_ref,
    image_ref,
    text_ref,
    image_out,
    text_out,
    loss_out,
    full,
    text,
    score,
    row_part,
    col_max,
    col_sum,
    stat,
    row_lse,
    col_lse,
    prob,
    visit_out,
    visit_in,
    part_out,
    part_in,
    text_send,
    loss_own,
    loss_in,
    relay_a,
    relay_b,
    send_sem,
    recv_sem,
    local_sem,
):
    d = lax.axis_index("dp")
    m = lax.axis_index("mp")
    c_m = m + 1 - 2 * lax.rem(m, 2)
    y_m = lax.rem(m + 2, 4)
    nxt = lax.rem(d + 1, n_dp)
    prv = lax.rem(d + n_dp - 1, n_dp)
    half = n_dp // 2
    swap = lax.div(d, half)
    out_swap = lax.div(lax.rem(d, half) + 1, half)
    back_swap = 1 - lax.div(lax.rem(d, half) + half - 1, half)
    to_c, to_y = (d, c_m), (d, y_m)
    to_next = (nxt, lax.rem(m + 2 * out_swap, 4))
    to_prev = (prv, lax.rem(m + 2 * back_swap, 4))
    place_in_half = lax.rem(d, half)
    first = place_in_half == 0
    relay = (place_in_half == 1) | (place_in_half == 4)
    base = d - place_in_half
    last = place_in_half == half - 1
    mine = lax.rem(m + 2 * swap, 4)
    other = lax.rem(c_m + 2 * swap, 4)
    mine_y = lax.rem(mine + 2, 4)
    other_y = lax.rem(other + 2, 4)

    def block(index, size=256):
        return pl.ds(pl.multiple_of(index * size, size), size)

    def remote(src, dst, index, device, arrival=None):
        return pltpu.make_async_remote_copy(
            src_ref=src,
            dst_ref=dst,
            send_sem=send_sem.at[index],
            recv_sem=recv_sem.at[index if arrival is None else arrival],
            device_id=device,
            device_id_type=MESH,
        )

    own, via = pl.ds(0, 256), pl.ds(256, 256)

    def piece(first, second, k):
        return block(2 * (first if k < 2 else second) + k % 2, 128)

    locals_ = [
        pltpu.make_async_copy(image_ref, full.at[:, own], local_sem.at[0]),
        pltpu.make_async_copy(text_ref.at[block(mine)], text.at[pl.ds(512, 256), own], local_sem.at[1]),
        pltpu.make_async_copy(text_ref.at[block(other)], text.at[pl.ds(768, 256), own], local_sem.at[2]),
    ]
    barrier = pltpu.get_barrier_semaphore()
    for device in (to_c, to_y, to_prev):
        pl.semaphore_signal(barrier, inc=1, device_id=device, device_id_type=MESH)

    @pl.when(place_in_half == 4)
    def _():
        pl.semaphore_signal(barrier, inc=1, device_id=(base, m), device_id_type=MESH)

    for copy in locals_:
        copy.start()

    @pl.when(first)
    def _():
        pl.semaphore_wait(barrier, 4)

    @pl.when(jnp.logical_not(first))
    def _():
        pl.semaphore_wait(barrier, 3)


    y_text = [
        remote(text_ref.at[piece(mine_y, other_y, k)], text.at[pl.ds(512 + 128 * k, 128), via], Y_T + k, to_y)
        for k in range(4)
    ]
    c_image = remote(image_ref, full.at[:, pl.ds(512, 256)], C_I, to_c)
    c_text = [
        remote(text_ref.at[block(other)], text.at[pl.ds(512, 256), pl.ds(512, 256)], C_T, to_c),
        remote(text_ref.at[block(mine)], text.at[pl.ds(768, 256), pl.ds(512, 256)], C_T + 1, to_c),
    ]
    c_via = [
        remote(
            text.at[pl.ds(512 + 128 * k, 128), via],
            text.at[pl.ds(512 + 128 * ((k + 2) % 4), 128), pl.ds(768, 256)],
            C_V + k,
            to_c,
        )
        for k in range(4)
    ]
    x_own = [
        remote(text_ref.at[piece(mine, other, k)], text.at[pl.ds(128 * k, 128), block(out_swap)], X_T + k, to_next)
        for k in range(4)
    ]
    x_via = [
        remote(
            text.at[pl.ds(512 + 128 * k, 128), via],
            text.at[pl.ds(128 * k, 128), block(1 - out_swap)],
            X_V + k,
            to_next,
        )
        for k in range(4)
    ]
    c_prev = [
        remote(
            text.at[pl.ds(128 * k, 128), pl.ds(0, 512)],
            text.at[pl.ds(128 * ((k + 2) % 4), 128), pl.ds(512, 512)],
            C_P + k,
            to_c,
        )
        for k in range(4)
    ]

    def y_image(r):
        return remote(image_ref.at[block(r, 128)], full.at[block(r, 128), via], Y_I + r, to_y)

    def c_forward(r):
        return remote(full.at[block(r, 128), via], full.at[block(r, 128), pl.ds(768, 256)], C_F + r, to_c)

    for k in range(4):
        y_text[k].start()
    for k in range(4):
        x_own[k].start()
    c_text[0].start()
    c_text[1].start()
    c_image.start()
    for r in range(CHUNKS):
        y_image(r).start()

    for k in range(4):
        y_text[k].wait_recv()
        x_via[k].start()
        c_via[k].start()
    for copy in locals_:
        copy.wait()
    for copy in [c_image] + c_text + c_via:
        copy.wait_recv()
    sent = y_text + [c_image] + c_text + c_via + x_own + x_via + c_prev

    factor = factor_ref[0]
    eye = lax.broadcasted_iota(jnp.int32, (128, 128), 0) == lax.broadcasted_iota(
        jnp.int32, (128, 128), 1
    )

    def arrive(p):
        for r in (2 * p, 2 * p + 1):
            y_image(r).wait_recv()
            c_forward(r).start()
        for r in (2 * p, 2 * p + 1):
            c_forward(r).wait_recv()

    def tile(t, p):
        scored = factor * dot_nt(text[512 * t : 512 * t + 512, :], full[block(p), :])
        score[p, 512 * t : 512 * t + 512, :] = scored
        top = jnp.max(scored, axis=0, keepdims=True)
        total = top + jnp.log(jnp.sum(jnp.exp(scored - top), axis=0, keepdims=True))
        for k in range(2):
            row_part[t, pl.ds(2 * p + k, 1), :] = total[:, 128 * k : 128 * k + 128]
        highest = jnp.max(scored, axis=1, keepdims=True)
        summed = jnp.sum(jnp.exp(scored - highest), axis=1, keepdims=True)
        for q in range(4):
            at = slice(128 * q, 128 * q + 128)
            col_max[p, 4 * t + q : 4 * t + q + 1, :] = jnp.sum(
                jnp.where(eye, highest[at], 0.0), axis=0, keepdims=True
            )
            col_sum[p, 4 * t + q : 4 * t + q + 1, :] = jnp.sum(
                jnp.where(eye, summed[at], 0.0), axis=0, keepdims=True
            )

    def own_chunk(p, carry):
        arrive(p)
        tile(1, p)
        return carry

    def prev_chunk(p, carry):
        tile(0, p)
        return carry

    def column(t):
        rows = slice(4 * t, 4 * t + 4)
        top = col_max[0, rows, :]
        for p in range(1, PAIRS):
            top = jnp.maximum(top, col_max[p, rows, :])
        total = jnp.zeros_like(top)
        for p in range(PAIRS):
            total = total + col_sum[p, rows, :] * jnp.exp(col_max[p, rows, :] - top)
        at = 2 - 2 * t
        stat[at, 0:4, :] = top + jnp.log(total)
        stat[at, 4:8, :] = jnp.zeros((4, 128), F32)

    to_n = remote(stat.at[0], stat.at[3], S_N, to_next)
    to_p = remote(stat.at[2], stat.at[1], S_P, to_prev)
    to_r = remote(stat.at[4], stat.at[5], S_R, to_y)

    early = jnp.where(first | last, PAIRS, 2)
    later = jnp.where(first | last, PAIRS, 3)
    lax.fori_loop(0, early, own_chunk, 0)

    @pl.when(first | last)
    def _():
        column(1)
        to_n.start()

    for k in range(4):
        x_own[k].wait_recv()
        x_via[k].wait_recv()
        c_prev[k].start()
    for k in range(4):
        c_prev[k].wait_recv()
    lax.fori_loop(0, early, prev_chunk, 0)
    lax.fori_loop(early, later, own_chunk, 0)
    lax.fori_loop(early, later, prev_chunk, 0)
    lax.fori_loop(later, PAIRS, own_chunk, 0)

    @pl.when(jnp.logical_not(first | last))
    def _():
        column(1)
        to_n.start()

    lax.fori_loop(later, PAIRS, prev_chunk, 0)
    stat[4] = log_add(row_part[0], row_part[1])
    to_r.start()
    column(0)
    to_p.start()
    sent += [to_n, to_p, to_r]

    place = [2 * mine, 2 * mine + 1, 2 * other, 2 * other + 1]

    def diagonal_block(q):
        pair = mine if q < 2 else other
        return score[pair, 512 + 128 * q : 640 + 128 * q, 128 * (q % 2) : 128 * (q % 2) + 128]

    diagonal = [
        jnp.sum(
            jnp.where(eye, diagonal_block(q), 0.0), axis=0, keepdims=True
        )
        for q in range(4)
    ]

    def spread(lse, at):
        for q in range(4):
            col_lse[at + 128 * q : at + 128 * q + 128, :] = jnp.broadcast_to(
                lse[q : q + 1, :], (128, 128)
            ).T

    to_p.wait_recv()
    lse_own = log_add(stat[0, 0:4, :], stat[1, 0:4, :])
    spread(lse_own, 512)
    to_r.wait_recv()
    row_lse[...] = log_add(stat[4], stat[5])
    for q in range(4):
        loss_own[q : q + 1, :] = (
            0.5 * (row_lse[pl.ds(place[q], 1), :] + lse_own[q : q + 1, :]) - diagonal[q]
        )
    loss_own[4:8, :] = jnp.zeros((4, 128), F32)
    loss_copy = remote(loss_own, loss_in, L_Y, to_y)
    unit = eye.astype(F32)

    def probability(p, k, q):
        at = slice(128 * q, 128 * q + 128)
        r = 2 * p + k
        scored = score[p, at, 128 * k : 128 * k + 128]
        row = row_lse[pl.ds(r, 1), :]
        value = 0.5 * (jnp.exp(scored - row) + jnp.exp(scored - col_lse[at, :]))
        if q >= 4:
            value = value - jnp.where(r == place[q - 4], unit, 0.0)
        prob[at, block(r, 128)] = value.astype(BF16)

    def own_probability(p, carry):
        for k in range(2):
            for q in range(4, 8):
                probability(p, k, q)
        return carry

    lax.fori_loop(0, jnp.where(first, PAIRS, 0), own_probability, 0)
    to_n.wait_recv()
    spread(log_add(stat[2, 0:4, :], stat[3, 0:4, :]), 0)

    def partial(r):
        return remote(part_out.at[block(r, 128)], part_in.at[block(r, 128)], G_Y + r, to_y)

    def relay_out(p):
        r = 2 * p + 1
        return remote(part_out.at[block(r, 128)], relay_a, G_Y + r, (base + 4 - 3 * p, m), R_A)

    passed = jnp.where(place_in_half == 1, 3, 1)
    relay_in = remote(relay_a, relay_a, R_A, to_y)
    relay_over = remote(relay_a, relay_b, R_B, to_y)
    relay_back = remote(relay_b, part_in.at[block(passed, 128)], R_A, (base, m), G_Y + passed)

    def prev_probability(p, carry):
        @pl.when(jnp.logical_not(first))
        def _():
            own_probability(p, 0)

        for k in range(2):
            for q in range(4):
                probability(p, k, q)
            lanes = block(2 * p + k, 128)
            part_out[lanes, :] = dot_tn(prob[:, lanes], text[:, 256:512]).astype(BF16)
            if k == 0:

                @pl.when(jnp.logical_not(relay & (p == 3)))
                def _():
                    partial(2 * p).start()

            else:

                @pl.when(first & (p < 2))
                def _():
                    relay_out(p).start()

                @pl.when(jnp.logical_not(first & (p < 2) | relay & (p == 3)))
                def _():
                    partial(2 * p + 1).start()

        return carry

    lax.fori_loop(0, PAIRS, prev_probability, 0)
    loss_copy.start()

    def visit(k):
        rows = pl.ds(256 * (k % 2), 256)
        kept = 1 - k // 2
        taken = lax.rem(kept + back_swap, 2)
        return remote(
            visit_out.at[rows, block(taken)], visit_in.at[rows, pl.ds(256 * kept, 256)], V_X + k, to_prev
        )

    def visiting(kept):
        lanes = block(lax.rem(kept + back_swap, 2))
        for rows in (slice(0, 256), slice(256, 512)):
            visit_out[rows, lanes] = dot_nn(prob[rows, :], full[:, lanes]).astype(BF16)

    visiting(1)
    visit(0).start()
    visit(1).start()

    @pl.when(relay)
    def _():
        relay_in.wait_recv()
        relay_over.start()
        partial(6).start()
        partial(7).start()

    visiting(0)

    @pl.when(jnp.logical_not(relay))
    def _():
        visit(2).start()
        visit(3).start()

    def image_final(i, carry):
        late = jnp.where(i < 2, 2 * i, jnp.where(i < 6, i + 2, 2 * i - 11))
        r = jnp.where(first, late, i)
        lanes = block(r, 128)
        value = dot_tn(prob[:, lanes], text[:, 0:256])
        partial(r).wait_recv()
        image_out[lanes, :] = (factor * (value + part_in[lanes, :].astype(F32))).astype(BF16)
        return carry

    def text_value(k):
        rows = slice(256 * (k % 2), 256 * (k % 2) + 256)
        lanes = slice(256, 512) if k < 2 else slice(0, 256)
        own_term = dot_nn(prob[512 + rows.start : 512 + rows.stop, :], full[:, lanes])
        visit(k).wait_recv()
        return (factor * (own_term + visit_in[rows, lanes].astype(F32))).astype(BF16)

    text_copies = []
    for k in range(2):
        rows = pl.ds(256 * k, 256)
        target = text_out.at[block(mine if k == 0 else other)]
        text_copies.append(remote(text_send.at[rows], target, T_Y + k, to_y))
    lax.fori_loop(0, 4, image_final, 0)
    for k in range(2):
        text_send[256 * k : 256 * k + 256, :] = text_value(k)
        text_copies[k].start()

    @pl.when(relay)
    def _():
        relay_over.wait_recv()
        relay_back.start()
        visit(2).start()
        visit(3).start()

    lax.fori_loop(4, CHUNKS, image_final, 0)
    for k in range(2):
        text_out[block(mine if k == 0 else other), :] = text_value(2 + k)

    loss_copy.wait_recv()
    loss_out[...] = jnp.where(swap == 1, loss_in[0:2, :], loss_own[0:2, :])
    for copy in sent + [loss_copy] + text_copies:
        copy.wait_send()

    @pl.when(relay)
    def _():
        relay_over.wait_send()
        relay_back.wait_send()

    for k in range(4):
        visit(k).wait_send()
    for r in range(CHUNKS):
        y_image(r).wait_send()
        c_forward(r).wait_send()
        partial(r).wait_send()
    for copy in text_copies:
        copy.wait_recv()


def finish(image_ref, text_ref, loss_ref, image_out, text_out, loss_out, sem):
    copies = []
    for k in range(4):
        rows = pl.ds(256 * k, 256)
        copies.append(pltpu.make_async_copy(image_ref.at[rows], image_out.at[rows], sem.at[k]))
        copies.append(pltpu.make_async_copy(text_ref.at[rows], text_out.at[rows], sem.at[4 + k]))
    for copy in copies:
        copy.start()
    for k in range(2):
        loss_out[pl.ds(128 * k, 128)] = loss_ref[k, :]
    for copy in copies:
        copy.wait()


def local(n_dp, image_emb, text_emb, logit_scale):
    vmem = pltpu.VMEM
    image_grad, text_grad, loss = pl.pallas_call(
        functools.partial(kernel, n_dp),
        out_shape=(
            vmem((1024, 256), BF16),
            vmem((1024, 256), BF16),
            vmem((2, 128), F32),
        ),
        in_specs=[
            pl.BlockSpec(memory_space=pltpu.SMEM),
            pl.BlockSpec(memory_space=pl.ANY),
            pl.BlockSpec(memory_space=pl.ANY),
        ],
        out_specs=[pl.BlockSpec(memory_space=vmem)] * 3,
        scratch_shapes=[
            vmem((1024, 1024), BF16),
            vmem((1024, 1024), BF16),
            vmem((PAIRS, 1024, 256), F32),
            vmem((2, 8, 128), F32),
            vmem((PAIRS, 8, 128), F32),
            vmem((PAIRS, 8, 128), F32),
            vmem((6, 8, 128), F32),
            vmem((8, 128), F32),
            vmem((1024, 128), F32),
            vmem((1024, 1024), BF16),
            vmem((512, 512), BF16),
            vmem((512, 512), BF16),
            vmem((1024, 256), BF16),
            vmem((1024, 256), BF16),
            vmem((512, 256), BF16),
            vmem((8, 128), F32),
            vmem((8, 128), F32),
            vmem((128, 256), BF16),
            vmem((128, 256), BF16),
            pltpu.SemaphoreType.DMA((N_COPIES,)),
            pltpu.SemaphoreType.DMA((N_COPIES,)),
            pltpu.SemaphoreType.DMA((3,)),
        ],
        compiler_params=pltpu.CompilerParams(
            collective_id=0, has_side_effects=True, vmem_limit_bytes=56 * 1024 * 1024
        ),
        cost_estimate=pl.CostEstimate(
            flops=4 * 2**31, bytes_accessed=2**21, transcendentals=2**22
        ),
    )(logit_scale, image_emb, text_emb)
    return pl.pallas_call(
        finish,
        out_shape=(
            jax.ShapeDtypeStruct((1024, 256), BF16),
            jax.ShapeDtypeStruct((1024, 256), BF16),
            jax.ShapeDtypeStruct((256,), F32),
        ),
        in_specs=[pl.BlockSpec(memory_space=vmem)] * 3,
        out_specs=[
            pl.BlockSpec(memory_space=pl.ANY),
            pl.BlockSpec(memory_space=pl.ANY),
            pl.BlockSpec(memory_space=vmem),
        ],
        scratch_shapes=[pltpu.SemaphoreType.DMA((8,))],
    )(*(pltpu.with_memory_space_constraint(x, vmem) for x in (image_grad, text_grad, loss)))


def solution(mesh):
    return jax.shard_map(
        functools.partial(local, mesh.shape["dp"]),
        mesh=mesh,
        in_specs=(P("dp", "mp"), P("dp", "mp"), P()),
        out_specs=(P("dp", "mp"), P("dp", "mp"), P(("dp", "mp"))),
        check_vma=False,
    )
```

```python
import functools

import jax
import jax.numpy as jnp
from jax import lax
from jax.experimental import pallas as pl
from jax.experimental.pallas import tpu as pltpu
from jax.sharding import PartitionSpec as P

MESH = pl.DeviceIdType.MESH
F32 = jnp.float32
BF16 = jnp.bfloat16
CHUNKS = 8
PAIRS = 4

Y_T = 0
Y_I = 4
C_I = 12
C_T = 13
C_V = 15
X_T = 19
X_V = 23
C_P = 27
C_F = 31
S_R = 39
S_N = 40
S_P = 41
V_X = 42
G_Y = 46
T_Y = 54
L_Y = 58
R_A = 59
R_B = 60
N_COPIES = 61


def dot_nt(a, b):
    return lax.dot_general(a, b, (((1,), (1,)), ((), ())), preferred_element_type=F32)


def dot_tn(a, b):
    return lax.dot_general(a, b, (((0,), (0,)), ((), ())), preferred_element_type=F32)


def dot_nn(a, b):
    return lax.dot_general(a, b, (((1,), (0,)), ((), ())), preferred_element_type=F32)


def log_add(a, b):
    top = jnp.maximum(a, b)
    return top + jnp.log(jnp.exp(a - top) + jnp.exp(b - top))


def kernel(
    n_dp,
    factor_ref,
    image_ref,
    text_ref,
    image_out,
    text_out,
    loss_out,
    full,
    text,
    score,
    row_part,
    col_max,
    col_sum,
    stat,
    row_lse,
    col_lse,
    prob,
    visit_out,
    visit_in,
    part_out,
    part_in,
    text_send,
    loss_own,
    loss_in,
    relay_a,
    relay_b,
    send_sem,
    recv_sem,
    local_sem,
):
    d = lax.axis_index("dp")
    m = lax.axis_index("mp")
    c_m = m + 1 - 2 * lax.rem(m, 2)
    y_m = lax.rem(m + 2, 4)
    nxt = lax.rem(d + 1, n_dp)
    prv = lax.rem(d + n_dp - 1, n_dp)
    half = n_dp // 2
    swap = lax.div(d, half)
    out_swap = lax.div(lax.rem(d, half) + 1, half)
    back_swap = 1 - lax.div(lax.rem(d, half) + half - 1, half)
    to_c, to_y = (d, c_m), (d, y_m)
    to_next = (nxt, lax.rem(m + 2 * out_swap, 4))
    to_prev = (prv, lax.rem(m + 2 * back_swap, 4))
    place_in_half = lax.rem(d, half)
    first = place_in_half == 0
    relay = (place_in_half == 1) | (place_in_half == 4)
    base = d - place_in_half
    last = place_in_half == half - 1
    mine = lax.rem(m + 2 * swap, 4)
    other = lax.rem(c_m + 2 * swap, 4)
    mine_y = lax.rem(mine + 2, 4)
    other_y = lax.rem(other + 2, 4)

    def block(index, size=256):
        return pl.ds(pl.multiple_of(index * size, size), size)

    def remote(src, dst, index, device, arrival=None):
        return pltpu.make_async_remote_copy(
            src_ref=src,
            dst_ref=dst,
            send_sem=send_sem.at[index],
            recv_sem=recv_sem.at[index if arrival is None else arrival],
            device_id=device,
            device_id_type=MESH,
        )

    own, via = pl.ds(0, 256), pl.ds(256, 256)

    def piece(first, second, k):
        return block(2 * (first if k < 2 else second) + k % 2, 128)

    locals_ = [
        pltpu.make_async_copy(image_ref, full.at[:, own], local_sem.at[0]),
        pltpu.make_async_copy(text_ref.at[block(mine)], text.at[pl.ds(512, 256), own], local_sem.at[1]),
        pltpu.make_async_copy(text_ref.at[block(other)], text.at[pl.ds(768, 256), own], local_sem.at[2]),
    ]
    barrier = pltpu.get_barrier_semaphore()
    for device in (to_c, to_y, to_prev):
        pl.semaphore_signal(barrier, inc=1, device_id=device, device_id_type=MESH)

    @pl.when(place_in_half == 4)
    def _():
        pl.semaphore_signal(barrier, inc=1, device_id=(base, m), device_id_type=MESH)

    for copy in locals_:
        copy.start()

    @pl.when(first)
    def _():
        pl.semaphore_wait(barrier, 4)

    @pl.when(jnp.logical_not(first))
    def _():
        pl.semaphore_wait(barrier, 3)


    y_text = [
        remote(text_ref.at[piece(mine_y, other_y, k)], text.at[pl.ds(512 + 128 * k, 128), via], Y_T + k, to_y)
        for k in range(4)
    ]
    c_image = remote(image_ref, full.at[:, pl.ds(512, 256)], C_I, to_c)
    c_text = [
        remote(text_ref.at[block(other)], text.at[pl.ds(512, 256), pl.ds(512, 256)], C_T, to_c),
        remote(text_ref.at[block(mine)], text.at[pl.ds(768, 256), pl.ds(512, 256)], C_T + 1, to_c),
    ]
    c_via = [
        remote(
            text.at[pl.ds(512 + 128 * k, 128), via],
            text.at[pl.ds(512 + 128 * ((k + 2) % 4), 128), pl.ds(768, 256)],
            C_V + k,
            to_c,
        )
        for k in range(4)
    ]
    x_own = [
        remote(text_ref.at[piece(mine, other, k)], text.at[pl.ds(128 * k, 128), block(out_swap)], X_T + k, to_next)
        for k in range(4)
    ]
    x_via = [
        remote(
            text.at[pl.ds(512 + 128 * k, 128), via],
            text.at[pl.ds(128 * k, 128), block(1 - out_swap)],
            X_V + k,
            to_next,
        )
        for k in range(4)
    ]
    c_prev = [
        remote(
            text.at[pl.ds(128 * k, 128), pl.ds(0, 512)],
            text.at[pl.ds(128 * ((k + 2) % 4), 128), pl.ds(512, 512)],
            C_P + k,
            to_c,
        )
        for k in range(4)
    ]

    def y_image(r):
        return remote(image_ref.at[block(r, 128)], full.at[block(r, 128), via], Y_I + r, to_y)

    def c_forward(r):
        return remote(full.at[block(r, 128), via], full.at[block(r, 128), pl.ds(768, 256)], C_F + r, to_c)

    for k in range(4):
        y_text[k].start()
    for k in range(4):
        x_own[k].start()
    c_text[0].start()
    c_text[1].start()
    c_image.start()
    for r in range(CHUNKS):
        y_image(r).start()

    for k in range(4):
        y_text[k].wait_recv()
        x_via[k].start()
        c_via[k].start()
    for copy in locals_:
        copy.wait()
    for copy in [c_image] + c_text + c_via:
        copy.wait_recv()
    sent = y_text + [c_image] + c_text + c_via + x_own + x_via + c_prev

    factor = factor_ref[0]
    eye = lax.broadcasted_iota(jnp.int32, (128, 128), 0) == lax.broadcasted_iota(
        jnp.int32, (128, 128), 1
    )

    def arrive(p, rows):
        for r in (2 * p, 2 * p + 1):
            y_image(r).wait_recv()
            c_forward(r).start()
        scored = dot_nt(text[rows, 0:768], full[block(p), 0:768])
        for r in (2 * p, 2 * p + 1):
            c_forward(r).wait_recv()
        return factor * (scored + dot_nt(text[rows, 768:1024], full[block(p), 768:1024]))

    def statistics(t, p, scored):
        score[p, 512 * t : 512 * t + 512, :] = scored
        top = jnp.max(scored, axis=0, keepdims=True)
        total = top + jnp.log(jnp.sum(jnp.exp(scored - top), axis=0, keepdims=True))
        for k in range(2):
            row_part[t, pl.ds(2 * p + k, 1), :] = total[:, 128 * k : 128 * k + 128]
        highest = jnp.max(scored, axis=1, keepdims=True)
        summed = jnp.sum(jnp.exp(scored - highest), axis=1, keepdims=True)
        for q in range(4):
            at = slice(128 * q, 128 * q + 128)
            col_max[p, 4 * t + q : 4 * t + q + 1, :] = jnp.sum(
                jnp.where(eye, highest[at], 0.0), axis=0, keepdims=True
            )
            col_sum[p, 4 * t + q : 4 * t + q + 1, :] = jnp.sum(
                jnp.where(eye, summed[at], 0.0), axis=0, keepdims=True
            )

    def own_chunk(p, carry):
        statistics(1, p, arrive(p, slice(512, 1024)))
        return carry

    def prev_chunk(p, carry):
        statistics(0, p, factor * dot_nt(text[0:512, :], full[block(p), :]))
        return carry

    def column(t):
        rows = slice(4 * t, 4 * t + 4)
        top = col_max[0, rows, :]
        for p in range(1, PAIRS):
            top = jnp.maximum(top, col_max[p, rows, :])
        total = jnp.zeros_like(top)
        for p in range(PAIRS):
            total = total + col_sum[p, rows, :] * jnp.exp(col_max[p, rows, :] - top)
        at = 2 - 2 * t
        stat[at, 0:4, :] = top + jnp.log(total)
        stat[at, 4:8, :] = jnp.zeros((4, 128), F32)

    to_n = remote(stat.at[0], stat.at[3], S_N, to_next)
    to_p = remote(stat.at[2], stat.at[1], S_P, to_prev)
    to_r = remote(stat.at[4], stat.at[5], S_R, to_y)

    early = jnp.where(first | last, PAIRS, 2)
    later = jnp.where(first | last, PAIRS, 3)
    lax.fori_loop(0, early, own_chunk, 0)

    @pl.when(first | last)
    def _():
        column(1)
        to_n.start()

    for k in range(4):
        x_own[k].wait_recv()
        x_via[k].wait_recv()
        c_prev[k].start()
    for k in range(4):
        c_prev[k].wait_recv()
    lax.fori_loop(0, early, prev_chunk, 0)
    lax.fori_loop(early, later, own_chunk, 0)
    lax.fori_loop(early, later, prev_chunk, 0)

    @pl.when(jnp.logical_not(first | last))
    def _():
        both = arrive(PAIRS - 1, slice(0, 1024))
        statistics(1, PAIRS - 1, both[512:1024, :])
        column(1)
        to_n.start()
        statistics(0, PAIRS - 1, both[0:512, :])

    stat[4] = log_add(row_part[0], row_part[1])
    to_r.start()
    column(0)
    to_p.start()
    sent += [to_n, to_p, to_r]

    place = [2 * mine, 2 * mine + 1, 2 * other, 2 * other + 1]

    def diagonal_block(q):
        pair = mine if q < 2 else other
        return score[pair, 512 + 128 * q : 640 + 128 * q, 128 * (q % 2) : 128 * (q % 2) + 128]

    diagonal = [
        jnp.sum(
            jnp.where(eye, diagonal_block(q), 0.0), axis=0, keepdims=True
        )
        for q in range(4)
    ]

    def spread(lse, at):
        for q in range(4):
            col_lse[at + 128 * q : at + 128 * q + 128, :] = jnp.broadcast_to(
                lse[q : q + 1, :], (128, 128)
            ).T

    to_p.wait_recv()
    lse_own = log_add(stat[0, 0:4, :], stat[1, 0:4, :])
    spread(lse_own, 512)
    to_r.wait_recv()
    row_lse[...] = log_add(stat[4], stat[5])
    loss_copy = remote(loss_own, loss_in, L_Y, to_y)
    unit = eye.astype(F32)

    def probability(p, k, q):
        at = slice(128 * q, 128 * q + 128)
        r = 2 * p + k
        scored = score[p, at, 128 * k : 128 * k + 128]
        row = row_lse[pl.ds(r, 1), :]
        value = 0.5 * (jnp.exp(scored - row) + jnp.exp(scored - col_lse[at, :]))
        if q >= 4:
            value = value - jnp.where(r == place[q - 4], unit, 0.0)
        prob[at, block(r, 128)] = value.astype(BF16)

    def own_probability(p, k):
        for q in range(4, 8):
            probability(p, k, q)

    def ahead(p, carry):
        own_probability(p, 0)
        own_probability(p, 1)
        return carry

    lax.fori_loop(0, jnp.where(first, PAIRS, 0), ahead, 0)
    to_n.wait_recv()
    spread(log_add(stat[2, 0:4, :], stat[3, 0:4, :]), 0)

    def partial(r):
        return remote(part_out.at[block(r, 128)], part_in.at[block(r, 128)], G_Y + r, to_y)

    def relay_out(p):
        r = 2 * p + 1
        return remote(part_out.at[block(r, 128)], relay_a, G_Y + r, (base + 4 - 3 * p, m), R_A)

    passed = jnp.where(place_in_half == 1, 3, 1)
    relay_in = remote(relay_a, relay_a, R_A, to_y)
    relay_over = remote(relay_a, relay_b, R_B, to_y)
    relay_back = remote(relay_b, part_in.at[block(passed, 128)], R_A, (base, m), G_Y + passed)

    def prev_probability(p, carry):
        for k in range(2):
            for q in range(4):
                probability(p, k, q)
        return carry

    def gradient(p, carry):
        for k in range(2):

            @pl.when(jnp.logical_not(first))
            def _():
                own_probability(p, k)

            lanes = block(2 * p + k, 128)
            part_out[lanes, :] = dot_tn(prob[:, lanes], text[:, 256:512]).astype(BF16)
            if k == 0:

                @pl.when(jnp.logical_not(relay & (p == 3)))
                def _():
                    partial(2 * p).start()

            else:

                @pl.when(first & (p < 2))
                def _():
                    relay_out(p).start()

                @pl.when(jnp.logical_not(first & (p < 2) | relay & (p == 3)))
                def _():
                    partial(2 * p + 1).start()

        return carry

    def visit(k):
        rows = pl.ds(256 * (k % 2), 256)
        kept = 1 - k // 2
        taken = lax.rem(kept + back_swap, 2)
        return remote(
            visit_out.at[rows, block(taken)], visit_in.at[rows, pl.ds(256 * kept, 256)], V_X + k, to_prev
        )

    def visiting(kept):
        lanes = block(lax.rem(kept + back_swap, 2))
        for rows in (slice(0, 256), slice(256, 512)):
            visit_out[rows, lanes] = dot_nn(prob[rows, :], full[:, lanes]).astype(BF16)

    prev_probability(0, 0)
    gradient(0, 0)
    lax.fori_loop(1, PAIRS, prev_probability, 0)
    visiting(1)
    visit(0).start()
    visit(1).start()
    gradient(1, 0)
    visiting(0)
    visit(2).start()

    @pl.when(jnp.logical_not(relay))
    def _():
        visit(3).start()

    lax.fori_loop(2, PAIRS, gradient, 0)
    for q in range(4):
        loss_own[q : q + 1, :] = (
            0.5 * (row_lse[pl.ds(place[q], 1), :] + lse_own[q : q + 1, :]) - diagonal[q]
        )
    loss_own[4:8, :] = jnp.zeros((4, 128), F32)
    loss_copy.start()

    @pl.when(relay)
    def _():
        relay_in.wait_recv()
        relay_over.start()
        partial(6).start()
        partial(7).start()

    def image_final(i, carry):
        late = jnp.where(i < 2, 2 * i, jnp.where(i < 6, i + 2, 2 * i - 11))
        r = jnp.where(first, late, i)
        lanes = block(r, 128)
        value = dot_tn(prob[:, lanes], text[:, 0:256])
        partial(r).wait_recv()
        image_out[lanes, :] = (factor * (value + part_in[lanes, :].astype(F32))).astype(BF16)
        return carry

    def text_value(k):
        rows = slice(256 * (k % 2), 256 * (k % 2) + 256)
        lanes = slice(256, 512) if k < 2 else slice(0, 256)
        own_term = dot_nn(prob[512 + rows.start : 512 + rows.stop, :], full[:, lanes])
        visit(k).wait_recv()
        return (factor * (own_term + visit_in[rows, lanes].astype(F32))).astype(BF16)

    text_copies = []
    for k in range(2):
        rows = pl.ds(256 * k, 256)
        target = text_out.at[block(mine if k == 0 else other)]
        text_copies.append(remote(text_send.at[rows], target, T_Y + k, to_y))
    lax.fori_loop(0, 4, image_final, 0)
    for k in range(2):
        text_send[256 * k : 256 * k + 256, :] = text_value(k)
        text_copies[k].start()

    @pl.when(relay)
    def _():
        relay_over.wait_recv()
        relay_back.start()
        visit(3).start()

    lax.fori_loop(4, CHUNKS, image_final, 0)
    for k in range(2):
        text_out[block(mine if k == 0 else other), :] = text_value(2 + k)

    loss_copy.wait_recv()
    loss_out[...] = jnp.where(swap == 1, loss_in[0:2, :], loss_own[0:2, :])
    for copy in sent + [loss_copy] + text_copies:
        copy.wait_send()

    @pl.when(relay)
    def _():
        relay_over.wait_send()
        relay_back.wait_send()

    for k in range(4):
        visit(k).wait_send()
    for r in range(CHUNKS):
        y_image(r).wait_send()
        c_forward(r).wait_send()
        partial(r).wait_send()
    for copy in text_copies:
        copy.wait_recv()


def finish(image_ref, text_ref, loss_ref, image_out, text_out, loss_out, sem):
    copies = []
    for k in range(4):
        rows = pl.ds(256 * k, 256)
        copies.append(pltpu.make_async_copy(image_ref.at[rows], image_out.at[rows], sem.at[k]))
        copies.append(pltpu.make_async_copy(text_ref.at[rows], text_out.at[rows], sem.at[4 + k]))
    for copy in copies:
        copy.start()
    for k in range(2):
        loss_out[pl.ds(128 * k, 128)] = loss_ref[k, :]
    for copy in copies:
        copy.wait()


def local(n_dp, image_emb, text_emb, logit_scale):
    vmem = pltpu.VMEM
    image_grad, text_grad, loss = pl.pallas_call(
        functools.partial(kernel, n_dp),
        out_shape=(
            vmem((1024, 256), BF16),
            vmem((1024, 256), BF16),
            vmem((2, 128), F32),
        ),
        in_specs=[
            pl.BlockSpec(memory_space=pltpu.SMEM),
            pl.BlockSpec(memory_space=pl.ANY),
            pl.BlockSpec(memory_space=pl.ANY),
        ],
        out_specs=[pl.BlockSpec(memory_space=vmem)] * 3,
        scratch_shapes=[
            vmem((1024, 1024), BF16),
            vmem((1024, 1024), BF16),
            vmem((PAIRS, 1024, 256), F32),
            vmem((2, 8, 128), F32),
            vmem((PAIRS, 8, 128), F32),
            vmem((PAIRS, 8, 128), F32),
            vmem((6, 8, 128), F32),
            vmem((8, 128), F32),
            vmem((1024, 128), F32),
            vmem((1024, 1024), BF16),
            vmem((512, 512), BF16),
            vmem((512, 512), BF16),
            vmem((1024, 256), BF16),
            vmem((1024, 256), BF16),
            vmem((512, 256), BF16),
            vmem((8, 128), F32),
            vmem((8, 128), F32),
            vmem((128, 256), BF16),
            vmem((128, 256), BF16),
            pltpu.SemaphoreType.DMA((N_COPIES,)),
            pltpu.SemaphoreType.DMA((N_COPIES,)),
            pltpu.SemaphoreType.DMA((3,)),
        ],
        compiler_params=pltpu.CompilerParams(
            collective_id=0, has_side_effects=True, vmem_limit_bytes=56 * 1024 * 1024
        ),
        cost_estimate=pl.CostEstimate(
            flops=4 * 2**31, bytes_accessed=2**21, transcendentals=2**22
        ),
    )(logit_scale, image_emb, text_emb)
    return pl.pallas_call(
        finish,
        out_shape=(
            jax.ShapeDtypeStruct((1024, 256), BF16),
            jax.ShapeDtypeStruct((1024, 256), BF16),
            jax.ShapeDtypeStruct((256,), F32),
        ),
        in_specs=[pl.BlockSpec(memory_space=vmem)] * 3,
        out_specs=[
            pl.BlockSpec(memory_space=pl.ANY),
            pl.BlockSpec(memory_space=pl.ANY),
            pl.BlockSpec(memory_space=vmem),
        ],
        scratch_shapes=[pltpu.SemaphoreType.DMA((8,))],
    )(*(pltpu.with_memory_space_constraint(x, vmem) for x in (image_grad, text_grad, loss)))


def solution(mesh):
    return jax.shard_map(
        functools.partial(local, mesh.shape["dp"]),
        mesh=mesh,
        in_specs=(P("dp", "mp"), P("dp", "mp"), P()),
        out_specs=(P("dp", "mp"), P("dp", "mp"), P(("dp", "mp"))),
        check_vma=False,
    )
```

```python
import functools

import jax
import jax.numpy as jnp
from jax import lax
from jax.experimental import pallas as pl
from jax.experimental.pallas import tpu as pltpu
from jax.sharding import PartitionSpec as P

MESH = pl.DeviceIdType.MESH
F32 = jnp.float32
BF16 = jnp.bfloat16
CHUNKS = 8
PAIRS = 4

Y_T = 0
Y_I = 4
C_I = 12
C_T = 13
C_V = 15
X_T = 19
X_V = 23
C_P = 27
C_F = 31
S_R = 39
S_N = 40
S_P = 41
V_X = 42
G_Y = 46
T_Y = 54
L_Y = 58
R_A = 59
R_B = 60
N_COPIES = 61


def dot_nt(a, b):
    return lax.dot_general(a, b, (((1,), (1,)), ((), ())), preferred_element_type=F32)


def dot_tn(a, b):
    return lax.dot_general(a, b, (((0,), (0,)), ((), ())), preferred_element_type=F32)


def dot_nn(a, b):
    return lax.dot_general(a, b, (((1,), (0,)), ((), ())), preferred_element_type=F32)


def log_add(a, b):
    top = jnp.maximum(a, b)
    return top + jnp.log(jnp.exp(a - top) + jnp.exp(b - top))


def kernel(
    n_dp,
    factor_ref,
    image_ref,
    text_ref,
    image_out,
    text_out,
    loss_out,
    full,
    text,
    score,
    row_part,
    col_max,
    col_sum,
    stat,
    row_lse,
    col_lse,
    prob,
    visit_out,
    visit_in,
    part_out,
    part_in,
    text_send,
    loss_own,
    loss_in,
    relay_a,
    relay_b,
    send_sem,
    recv_sem,
    local_sem,
):
    d = lax.axis_index("dp")
    m = lax.axis_index("mp")
    c_m = m + 1 - 2 * lax.rem(m, 2)
    y_m = lax.rem(m + 2, 4)
    nxt = lax.rem(d + 1, n_dp)
    prv = lax.rem(d + n_dp - 1, n_dp)
    half = n_dp // 2
    swap = lax.div(d, half)
    out_swap = lax.div(lax.rem(d, half) + 1, half)
    back_swap = 1 - lax.div(lax.rem(d, half) + half - 1, half)
    to_c, to_y = (d, c_m), (d, y_m)
    to_next = (nxt, lax.rem(m + 2 * out_swap, 4))
    to_prev = (prv, lax.rem(m + 2 * back_swap, 4))
    place_in_half = lax.rem(d, half)
    first = place_in_half == 0
    relay = (place_in_half == 1) | (place_in_half == 4)
    base = d - place_in_half
    last = place_in_half == half - 1
    mine = lax.rem(m + 2 * swap, 4)
    other = lax.rem(c_m + 2 * swap, 4)
    mine_y = lax.rem(mine + 2, 4)
    other_y = lax.rem(other + 2, 4)

    def block(index, size=256):
        return pl.ds(pl.multiple_of(index * size, size), size)

    def remote(src, dst, index, device, arrival=None):
        return pltpu.make_async_remote_copy(
            src_ref=src,
            dst_ref=dst,
            send_sem=send_sem.at[index],
            recv_sem=recv_sem.at[index if arrival is None else arrival],
            device_id=device,
            device_id_type=MESH,
        )

    own, via = pl.ds(0, 256), pl.ds(256, 256)

    def piece(first, second, k):
        return block(2 * (first if k < 2 else second) + k % 2, 128)

    locals_ = [
        pltpu.make_async_copy(image_ref, full.at[:, own], local_sem.at[0]),
        pltpu.make_async_copy(text_ref.at[block(mine)], text.at[pl.ds(512, 256), own], local_sem.at[1]),
        pltpu.make_async_copy(text_ref.at[block(other)], text.at[pl.ds(768, 256), own], local_sem.at[2]),
    ]
    barrier = pltpu.get_barrier_semaphore()
    for device in (to_c, to_y, to_prev):
        pl.semaphore_signal(barrier, inc=1, device_id=device, device_id_type=MESH)

    @pl.when(place_in_half == 4)
    def _():
        pl.semaphore_signal(barrier, inc=1, device_id=(base, m), device_id_type=MESH)

    for copy in locals_:
        copy.start()

    @pl.when(first)
    def _():
        pl.semaphore_wait(barrier, 4)

    @pl.when(jnp.logical_not(first))
    def _():
        pl.semaphore_wait(barrier, 3)


    y_text = [
        remote(text_ref.at[piece(mine_y, other_y, k)], text.at[pl.ds(512 + 128 * k, 128), via], Y_T + k, to_y)
        for k in range(4)
    ]
    c_image = remote(image_ref, full.at[:, pl.ds(512, 256)], C_I, to_c)
    c_text = [
        remote(text_ref.at[block(other)], text.at[pl.ds(512, 256), pl.ds(512, 256)], C_T, to_c),
        remote(text_ref.at[block(mine)], text.at[pl.ds(768, 256), pl.ds(512, 256)], C_T + 1, to_c),
    ]
    c_via = [
        remote(
            text.at[pl.ds(512 + 128 * k, 128), via],
            text.at[pl.ds(512 + 128 * ((k + 2) % 4), 128), pl.ds(768, 256)],
            C_V + k,
            to_c,
        )
        for k in range(4)
    ]
    x_own = [
        remote(text_ref.at[piece(mine, other, k)], text.at[pl.ds(128 * k, 128), block(out_swap)], X_T + k, to_next)
        for k in range(4)
    ]
    x_via = [
        remote(
            text.at[pl.ds(512 + 128 * k, 128), via],
            text.at[pl.ds(128 * k, 128), block(1 - out_swap)],
            X_V + k,
            to_next,
        )
        for k in range(4)
    ]
    c_prev = [
        remote(
            text.at[pl.ds(128 * k, 128), pl.ds(0, 512)],
            text.at[pl.ds(128 * ((k + 2) % 4), 128), pl.ds(512, 512)],
            C_P + k,
            to_c,
        )
        for k in range(4)
    ]

    def y_image(r):
        return remote(image_ref.at[block(r, 128)], full.at[block(r, 128), via], Y_I + r, to_y)

    def c_forward(r):
        return remote(full.at[block(r, 128), via], full.at[block(r, 128), pl.ds(768, 256)], C_F + r, to_c)

    for k in range(4):
        y_text[k].start()
    for k in range(4):
        x_own[k].start()
    c_text[0].start()
    c_text[1].start()
    c_image.start()
    for r in range(CHUNKS):
        y_image(r).start()

    for k in range(4):
        y_text[k].wait_recv()
        x_via[k].start()
        c_via[k].start()
    for copy in locals_:
        copy.wait()
    for copy in [c_image] + c_text + c_via:
        copy.wait_recv()
    sent = y_text + [c_image] + c_text + c_via + x_own + x_via + c_prev

    factor = factor_ref[0]
    eye = lax.broadcasted_iota(jnp.int32, (128, 128), 0) == lax.broadcasted_iota(
        jnp.int32, (128, 128), 1
    )

    def arrive(p, rows):
        for r in (2 * p, 2 * p + 1):
            y_image(r).wait_recv()
            c_forward(r).start()
        scored = dot_nt(text[rows, 0:768], full[block(p), 0:768])
        for r in (2 * p, 2 * p + 1):
            c_forward(r).wait_recv()
        return factor * (scored + dot_nt(text[rows, 768:1024], full[block(p), 768:1024]))

    def statistics(t, p, scored):
        score[p, 512 * t : 512 * t + 512, :] = scored
        top = jnp.max(scored, axis=0, keepdims=True)
        total = top + jnp.log(jnp.sum(jnp.exp(scored - top), axis=0, keepdims=True))
        for k in range(2):
            row_part[t, pl.ds(2 * p + k, 1), :] = total[:, 128 * k : 128 * k + 128]
        highest = jnp.max(scored, axis=1, keepdims=True)
        summed = jnp.sum(jnp.exp(scored - highest), axis=1, keepdims=True)
        for q in range(4):
            at = slice(128 * q, 128 * q + 128)
            col_max[p, 4 * t + q : 4 * t + q + 1, :] = jnp.sum(
                jnp.where(eye, highest[at], 0.0), axis=0, keepdims=True
            )
            col_sum[p, 4 * t + q : 4 * t + q + 1, :] = jnp.sum(
                jnp.where(eye, summed[at], 0.0), axis=0, keepdims=True
            )

    def own_chunk(p, carry):
        statistics(1, p, arrive(p, slice(512, 1024)))
        return carry

    def prev_chunk(p, carry):
        statistics(0, p, factor * dot_nt(text[0:512, :], full[block(p), :]))
        return carry

    def column(t):
        rows = slice(4 * t, 4 * t + 4)
        top = col_max[0, rows, :]
        for p in range(1, PAIRS):
            top = jnp.maximum(top, col_max[p, rows, :])
        total = jnp.zeros_like(top)
        for p in range(PAIRS):
            total = total + col_sum[p, rows, :] * jnp.exp(col_max[p, rows, :] - top)
        at = 2 - 2 * t
        stat[at, 0:4, :] = top + jnp.log(total)
        stat[at, 4:8, :] = jnp.zeros((4, 128), F32)

    to_n = remote(stat.at[0], stat.at[3], S_N, to_next)
    to_p = remote(stat.at[2], stat.at[1], S_P, to_prev)
    to_r = remote(stat.at[4], stat.at[5], S_R, to_y)

    early = jnp.where(first | last, PAIRS, 2)
    later = jnp.where(first | last, PAIRS, 3)
    lax.fori_loop(0, early, own_chunk, 0)

    @pl.when(first | last)
    def _():
        column(1)
        to_n.start()

    for k in range(4):
        x_own[k].wait_recv()
        x_via[k].wait_recv()
        c_prev[k].start()
    for k in range(4):
        c_prev[k].wait_recv()
    lax.fori_loop(0, early, prev_chunk, 0)
    lax.fori_loop(early, later, own_chunk, 0)
    lax.fori_loop(early, later, prev_chunk, 0)

    @pl.when(jnp.logical_not(first | last))
    def _():
        both = arrive(PAIRS - 1, slice(0, 1024))
        statistics(1, PAIRS - 1, both[512:1024, :])
        column(1)
        to_n.start()
        statistics(0, PAIRS - 1, both[0:512, :])

    stat[4] = log_add(row_part[0], row_part[1])
    to_r.start()
    column(0)
    to_p.start()
    sent += [to_n, to_p, to_r]

    place = [2 * mine, 2 * mine + 1, 2 * other, 2 * other + 1]

    def diagonal_block(q):
        pair = mine if q < 2 else other
        return score[pair, 512 + 128 * q : 640 + 128 * q, 128 * (q % 2) : 128 * (q % 2) + 128]

    diagonal = [
        jnp.sum(
            jnp.where(eye, diagonal_block(q), 0.0), axis=0, keepdims=True
        )
        for q in range(4)
    ]

    def spread(lse, at):
        for q in range(4):
            col_lse[at + 128 * q : at + 128 * q + 128, :] = jnp.broadcast_to(
                lse[q : q + 1, :], (128, 128)
            ).T

    to_p.wait_recv()
    lse_own = log_add(stat[0, 0:4, :], stat[1, 0:4, :])
    spread(lse_own, 512)
    to_r.wait_recv()
    row_lse[...] = log_add(stat[4], stat[5])
    loss_copy = remote(loss_own, loss_in, L_Y, to_y)
    unit = eye.astype(F32)

    def probability(p, k, q):
        at = slice(128 * q, 128 * q + 128)
        r = 2 * p + k
        scored = score[p, at, 128 * k : 128 * k + 128]
        row = row_lse[pl.ds(r, 1), :]
        value = 0.5 * (jnp.exp(scored - row) + jnp.exp(scored - col_lse[at, :]))
        if q >= 4:
            value = value - jnp.where(r == place[q - 4], unit, 0.0)
        prob[at, block(r, 128)] = value.astype(BF16)

    def own_probability(p, k):
        for q in range(4, 8):
            probability(p, k, q)

    def ahead(p, carry):
        own_probability(p, 0)
        own_probability(p, 1)
        return carry

    lax.fori_loop(0, jnp.where(first, PAIRS, 0), ahead, 0)
    to_n.wait_recv()
    spread(log_add(stat[2, 0:4, :], stat[3, 0:4, :]), 0)

    def partial(r):
        return remote(part_out.at[block(r, 128)], part_in.at[block(r, 128)], G_Y + r, to_y)

    def relay_out(p):
        r = 2 * p + 1
        return remote(part_out.at[block(r, 128)], relay_a, G_Y + r, (base + 4 - 3 * p, m), R_A)

    passed = jnp.where(place_in_half == 1, 3, 1)
    relay_in = remote(relay_a, relay_a, R_A, to_y)
    relay_over = remote(relay_a, relay_b, R_B, to_y)
    relay_back = remote(relay_b, part_in.at[block(passed, 128)], R_A, (base, m), G_Y + passed)

    def prev_probability(p, carry):
        for k in range(2):
            for q in range(4):
                probability(p, k, q)
        return carry

    def gradient(p, carry):
        for k in range(2):

            @pl.when(jnp.logical_not(first))
            def _():
                own_probability(p, k)

            lanes = block(2 * p + k, 128)
            part_out[lanes, :] = dot_tn(prob[:, lanes], text[:, 256:512]).astype(BF16)
            if k == 0:

                @pl.when(jnp.logical_not(relay & (p == 3)))
                def _():
                    partial(2 * p).start()

            else:

                @pl.when(first & (p < 2))
                def _():
                    relay_out(p).start()

                @pl.when(jnp.logical_not(first & (p < 2) | relay & (p == 3)))
                def _():
                    partial(2 * p + 1).start()

        return carry

    def visit(k):
        rows = pl.ds(256 * (k % 2), 256)
        kept = 1 - k // 2
        taken = lax.rem(kept + back_swap, 2)
        return remote(
            visit_out.at[rows, block(taken)], visit_in.at[rows, pl.ds(256 * kept, 256)], V_X + k, to_prev
        )

    def visiting(kept):
        lanes = block(lax.rem(kept + back_swap, 2))
        for rows in (slice(0, 256), slice(256, 512)):
            visit_out[rows, lanes] = dot_nn(prob[rows, :], full[:, lanes]).astype(BF16)

    prev_probability(0, 0)
    gradient(0, 0)
    lax.fori_loop(1, PAIRS, prev_probability, 0)
    visiting(1)
    visit(0).start()
    visit(1).start()
    gradient(1, 0)
    visiting(0)
    visit(2).start()

    @pl.when(jnp.logical_not(relay))
    def _():
        visit(3).start()

    lax.fori_loop(2, PAIRS, gradient, 0)
    for q in range(4):
        loss_own[q : q + 1, :] = (
            0.5 * (row_lse[pl.ds(place[q], 1), :] + lse_own[q : q + 1, :]) - diagonal[q]
        )
    loss_own[4:8, :] = jnp.zeros((4, 128), F32)
    loss_copy.start()

    @pl.when(relay)
    def _():
        relay_in.wait_recv()
        relay_over.start()
        partial(6).start()
        partial(7).start()

    def image_final(i, carry):
        late = jnp.where(i < 2, 2 * i, jnp.where(i < 6, i + 2, 2 * i - 11))
        r = jnp.where(first, late, i)
        lanes = block(r, 128)
        value = dot_tn(prob[:, lanes], text[:, 0:256])
        partial(r).wait_recv()
        image_out[lanes, :] = (factor * (value + part_in[lanes, :].astype(F32))).astype(BF16)
        return carry

    def text_value(k):
        rows = slice(256 * (k % 2), 256 * (k % 2) + 256)
        lanes = slice(256, 512) if k < 2 else slice(0, 256)
        own_term = dot_nn(prob[512 + rows.start : 512 + rows.stop, :], full[:, lanes])
        visit(k).wait_recv()
        return (factor * (own_term + visit_in[rows, lanes].astype(F32))).astype(BF16)

    text_copies = []
    for k in range(2):
        rows = pl.ds(256 * k, 256)
        target = text_out.at[block(mine if k == 0 else other)]
        text_copies.append(remote(text_send.at[rows], target, T_Y + k, to_y))
    lax.fori_loop(0, 4, image_final, 0)
    for k in range(2):
        text_send[256 * k : 256 * k + 256, :] = text_value(k)
        text_copies[k].start()

    @pl.when(relay)
    def _():
        relay_over.wait_recv()
        relay_back.start()
        visit(3).start()

    lax.fori_loop(4, CHUNKS, image_final, 0)
    for k in range(2):
        text_out[block(mine if k == 0 else other), :] = text_value(2 + k)

    loss_copy.wait_recv()
    loss_out[...] = jnp.where(swap == 1, loss_in[0:2, :], loss_own[0:2, :])
    for copy in sent + [loss_copy] + text_copies:
        copy.wait_send()

    @pl.when(relay)
    def _():
        relay_over.wait_send()
        relay_back.wait_send()

    for k in range(4):
        visit(k).wait_send()
    for r in range(CHUNKS):
        y_image(r).wait_send()
        c_forward(r).wait_send()
        partial(r).wait_send()
    for copy in text_copies:
        copy.wait_recv()


def finish(image_ref, text_ref, loss_ref, image_out, text_out, loss_out, loss, sem):
    copies = []
    for k in range(4):
        rows = pl.ds(256 * k, 256)
        copies.append(pltpu.make_async_copy(image_ref.at[rows], image_out.at[rows], sem.at[k]))
        copies.append(pltpu.make_async_copy(text_ref.at[rows], text_out.at[rows], sem.at[4 + k]))
    for copy in copies:
        copy.start()
    for k in range(2):
        loss[pl.ds(128 * k, 128)] = loss_ref[k, :]
    copies.append(pltpu.make_async_copy(loss, loss_out, sem.at[8]))
    copies[-1].start()
    for copy in copies:
        copy.wait()


def local(n_dp, image_emb, text_emb, logit_scale):
    vmem = pltpu.VMEM
    image_grad, text_grad, loss = pl.pallas_call(
        functools.partial(kernel, n_dp),
        out_shape=(
            vmem((1024, 256), BF16),
            vmem((1024, 256), BF16),
            vmem((2, 128), F32),
        ),
        in_specs=[
            pl.BlockSpec(memory_space=pltpu.SMEM),
            pl.BlockSpec(memory_space=pl.ANY),
            pl.BlockSpec(memory_space=pl.ANY),
        ],
        out_specs=[pl.BlockSpec(memory_space=vmem)] * 3,
        scratch_shapes=[
            vmem((1024, 1024), BF16),
            vmem((1024, 1024), BF16),
            vmem((PAIRS, 1024, 256), F32),
            vmem((2, 8, 128), F32),
            vmem((PAIRS, 8, 128), F32),
            vmem((PAIRS, 8, 128), F32),
            vmem((6, 8, 128), F32),
            vmem((8, 128), F32),
            vmem((1024, 128), F32),
            vmem((1024, 1024), BF16),
            vmem((512, 512), BF16),
            vmem((512, 512), BF16),
            vmem((1024, 256), BF16),
            vmem((1024, 256), BF16),
            vmem((512, 256), BF16),
            vmem((8, 128), F32),
            vmem((8, 128), F32),
            vmem((128, 256), BF16),
            vmem((128, 256), BF16),
            pltpu.SemaphoreType.DMA((N_COPIES,)),
            pltpu.SemaphoreType.DMA((N_COPIES,)),
            pltpu.SemaphoreType.DMA((3,)),
        ],
        compiler_params=pltpu.CompilerParams(
            collective_id=0, has_side_effects=True, vmem_limit_bytes=56 * 1024 * 1024
        ),
        cost_estimate=pl.CostEstimate(
            flops=4 * 2**31, bytes_accessed=2**21, transcendentals=2**22
        ),
    )(logit_scale, image_emb, text_emb)
    return pl.pallas_call(
        finish,
        out_shape=(
            jax.ShapeDtypeStruct((1024, 256), BF16),
            jax.ShapeDtypeStruct((1024, 256), BF16),
            jax.ShapeDtypeStruct((256,), F32),
        ),
        in_specs=[pl.BlockSpec(memory_space=vmem)] * 3,
        out_specs=[pl.BlockSpec(memory_space=pl.ANY)] * 3,
        scratch_shapes=[vmem((256,), F32), pltpu.SemaphoreType.DMA((9,))],
    )(*(pltpu.with_memory_space_constraint(x, vmem) for x in (image_grad, text_grad, loss)))


def solution(mesh):
    return jax.shard_map(
        functools.partial(local, mesh.shape["dp"]),
        mesh=mesh,
        in_specs=(P("dp", "mp"), P("dp", "mp"), P()),
        out_specs=(P("dp", "mp"), P("dp", "mp"), P(("dp", "mp"))),
        check_vma=False,
    )
```

```python
import functools

import jax
import jax.numpy as jnp
from jax import lax
from jax.experimental import pallas as pl
from jax.experimental.pallas import tpu as pltpu
from jax.sharding import PartitionSpec as P

MESH = pl.DeviceIdType.MESH
F32 = jnp.float32
BF16 = jnp.bfloat16
CHUNKS = 8
PAIRS = 4

Y_T = 0
Y_I = 4
C_I = 12
C_T = 13
C_V = 15
X_T = 19
X_V = 23
C_P = 27
C_F = 31
S_R = 39
S_N = 40
S_P = 41
V_X = 42
G_Y = 46
T_Y = 54
L_Y = 58
R_A = 59
R_B = 60
N_COPIES = 61


def dot_nt(a, b):
    return lax.dot_general(a, b, (((1,), (1,)), ((), ())), preferred_element_type=F32)


def dot_tn(a, b):
    return lax.dot_general(a, b, (((0,), (0,)), ((), ())), preferred_element_type=F32)


def dot_nn(a, b):
    return lax.dot_general(a, b, (((1,), (0,)), ((), ())), preferred_element_type=F32)


def log_add(a, b):
    top = jnp.maximum(a, b)
    return top + jnp.log(jnp.exp(a - top) + jnp.exp(b - top))


def kernel(
    n_dp,
    factor_ref,
    image_ref,
    text_ref,
    image_out,
    text_out,
    loss_out,
    full,
    text,
    score,
    row_part,
    col_max,
    col_sum,
    stat,
    row_lse,
    col_lse,
    prob,
    visit_out,
    visit_in,
    part_out,
    part_in,
    text_send,
    loss_own,
    loss_in,
    relay_a,
    relay_b,
    send_sem,
    recv_sem,
    local_sem,
):
    d = lax.axis_index("dp")
    m = lax.axis_index("mp")
    c_m = m + 1 - 2 * lax.rem(m, 2)
    y_m = lax.rem(m + 2, 4)
    nxt = lax.rem(d + 1, n_dp)
    prv = lax.rem(d + n_dp - 1, n_dp)
    half = n_dp // 2
    swap = lax.div(d, half)
    out_swap = lax.div(lax.rem(d, half) + 1, half)
    back_swap = 1 - lax.div(lax.rem(d, half) + half - 1, half)
    to_c, to_y = (d, c_m), (d, y_m)
    to_next = (nxt, lax.rem(m + 2 * out_swap, 4))
    to_prev = (prv, lax.rem(m + 2 * back_swap, 4))
    place_in_half = lax.rem(d, half)
    first = place_in_half == 0
    relay = (place_in_half == 1) | (place_in_half == 4)
    base = d - place_in_half
    last = place_in_half == half - 1
    mine = lax.rem(m + 2 * swap, 4)
    other = lax.rem(c_m + 2 * swap, 4)
    mine_y = lax.rem(mine + 2, 4)
    other_y = lax.rem(other + 2, 4)

    def block(index, size=256):
        return pl.ds(pl.multiple_of(index * size, size), size)

    def remote(src, dst, index, device, arrival=None):
        return pltpu.make_async_remote_copy(
            src_ref=src,
            dst_ref=dst,
            send_sem=send_sem.at[index],
            recv_sem=recv_sem.at[index if arrival is None else arrival],
            device_id=device,
            device_id_type=MESH,
        )

    own, via = pl.ds(0, 256), pl.ds(256, 256)

    def piece(first, second, k):
        return block(2 * (first if k < 2 else second) + k % 2, 128)

    locals_ = [
        pltpu.make_async_copy(image_ref, full.at[:, own], local_sem.at[0]),
        pltpu.make_async_copy(text_ref.at[block(mine)], text.at[pl.ds(512, 256), own], local_sem.at[1]),
        pltpu.make_async_copy(text_ref.at[block(other)], text.at[pl.ds(768, 256), own], local_sem.at[2]),
    ]
    barrier = pltpu.get_barrier_semaphore()
    for device in (to_c, to_y, to_prev):
        pl.semaphore_signal(barrier, inc=1, device_id=device, device_id_type=MESH)

    @pl.when(place_in_half == 4)
    def _():
        pl.semaphore_signal(barrier, inc=1, device_id=(base, m), device_id_type=MESH)

    for copy in locals_:
        copy.start()

    @pl.when(first)
    def _():
        pl.semaphore_wait(barrier, 4)

    @pl.when(jnp.logical_not(first))
    def _():
        pl.semaphore_wait(barrier, 3)


    y_text = [
        remote(text_ref.at[piece(mine_y, other_y, k)], text.at[pl.ds(512 + 128 * k, 128), via], Y_T + k, to_y)
        for k in range(4)
    ]
    c_image = remote(image_ref, full.at[:, pl.ds(512, 256)], C_I, to_c)
    c_text = [
        remote(text_ref.at[block(other)], text.at[pl.ds(512, 256), pl.ds(512, 256)], C_T, to_c),
        remote(text_ref.at[block(mine)], text.at[pl.ds(768, 256), pl.ds(512, 256)], C_T + 1, to_c),
    ]
    c_via = [
        remote(
            text.at[pl.ds(512 + 128 * k, 128), via],
            text.at[pl.ds(512 + 128 * ((k + 2) % 4), 128), pl.ds(768, 256)],
            C_V + k,
            to_c,
        )
        for k in range(4)
    ]
    x_own = [
        remote(text_ref.at[piece(mine, other, k)], text.at[pl.ds(128 * k, 128), block(out_swap)], X_T + k, to_next)
        for k in range(4)
    ]
    x_via = [
        remote(
            text.at[pl.ds(512 + 128 * k, 128), via],
            text.at[pl.ds(128 * k, 128), block(1 - out_swap)],
            X_V + k,
            to_next,
        )
        for k in range(4)
    ]
    c_prev = [
        remote(
            text.at[pl.ds(128 * k, 128), pl.ds(0, 512)],
            text.at[pl.ds(128 * ((k + 2) % 4), 128), pl.ds(512, 512)],
            C_P + k,
            to_c,
        )
        for k in range(4)
    ]

    def y_image(r):
        return remote(image_ref.at[block(r, 128)], full.at[block(r, 128), via], Y_I + r, to_y)

    def c_forward(r):
        return remote(full.at[block(r, 128), via], full.at[block(r, 128), pl.ds(768, 256)], C_F + r, to_c)

    for k in range(4):
        y_text[k].start()
    for k in range(4):
        x_own[k].start()
    c_text[0].start()
    c_text[1].start()
    c_image.start()
    for r in range(CHUNKS):
        y_image(r).start()

    for k in range(4):
        y_text[k].wait_recv()
        x_via[k].start()
        c_via[k].start()
    for copy in locals_:
        copy.wait()
    for copy in [c_image] + c_text + c_via:
        copy.wait_recv()
    sent = y_text + [c_image] + c_text + c_via + x_own + x_via + c_prev

    factor = factor_ref[0]
    eye = lax.broadcasted_iota(jnp.int32, (128, 128), 0) == lax.broadcasted_iota(
        jnp.int32, (128, 128), 1
    )

    def arrive(p, rows):
        for r in (2 * p, 2 * p + 1):
            y_image(r).wait_recv()
            c_forward(r).start()
        scored = dot_nt(text[rows, 0:768], full[block(p), 0:768])
        for r in (2 * p, 2 * p + 1):
            c_forward(r).wait_recv()
        return factor * (scored + dot_nt(text[rows, 768:1024], full[block(p), 768:1024]))

    def statistics(t, p, scored):
        score[p, 512 * t : 512 * t + 512, :] = scored
        top = jnp.max(scored, axis=0, keepdims=True)
        total = top + jnp.log(jnp.sum(jnp.exp(scored - top), axis=0, keepdims=True))
        for k in range(2):
            row_part[t, pl.ds(2 * p + k, 1), :] = total[:, 128 * k : 128 * k + 128]
        highest = jnp.max(scored, axis=1, keepdims=True)
        summed = jnp.sum(jnp.exp(scored - highest), axis=1, keepdims=True)
        for q in range(4):
            at = slice(128 * q, 128 * q + 128)
            col_max[p, 4 * t + q : 4 * t + q + 1, :] = jnp.sum(
                jnp.where(eye, highest[at], 0.0), axis=0, keepdims=True
            )
            col_sum[p, 4 * t + q : 4 * t + q + 1, :] = jnp.sum(
                jnp.where(eye, summed[at], 0.0), axis=0, keepdims=True
            )

    def own_chunk(p, carry):
        statistics(1, p, arrive(p, slice(512, 1024)))
        return carry

    def prev_chunk(p, carry):
        statistics(0, p, factor * dot_nt(text[0:512, :], full[block(p), :]))
        return carry

    def column(t):
        rows = slice(4 * t, 4 * t + 4)
        top = col_max[0, rows, :]
        for p in range(1, PAIRS):
            top = jnp.maximum(top, col_max[p, rows, :])
        total = jnp.zeros_like(top)
        for p in range(PAIRS):
            total = total + col_sum[p, rows, :] * jnp.exp(col_max[p, rows, :] - top)
        at = 2 - 2 * t
        stat[at, 0:4, :] = top + jnp.log(total)
        stat[at, 4:8, :] = jnp.zeros((4, 128), F32)

    to_n = remote(stat.at[0], stat.at[3], S_N, to_next)
    to_p = remote(stat.at[2], stat.at[1], S_P, to_prev)
    to_r = remote(stat.at[4], stat.at[5], S_R, to_y)

    early = jnp.where(first | last, PAIRS, 2)
    later = jnp.where(first | last, PAIRS, 3)
    lax.fori_loop(0, early, own_chunk, 0)

    @pl.when(first | last)
    def _():
        column(1)
        to_n.start()

    for k in range(4):
        x_own[k].wait_recv()
        x_via[k].wait_recv()
        c_prev[k].start()
    for k in range(4):
        c_prev[k].wait_recv()
    lax.fori_loop(0, early, prev_chunk, 0)
    lax.fori_loop(early, later, own_chunk, 0)
    lax.fori_loop(early, later, prev_chunk, 0)

    @pl.when(jnp.logical_not(first | last))
    def _():
        both = arrive(PAIRS - 1, slice(0, 1024))
        statistics(1, PAIRS - 1, both[512:1024, :])
        column(1)
        to_n.start()
        statistics(0, PAIRS - 1, both[0:512, :])

    stat[4] = log_add(row_part[0], row_part[1])
    to_r.start()
    column(0)
    to_p.start()
    sent += [to_n, to_p, to_r]

    place = [2 * mine, 2 * mine + 1, 2 * other, 2 * other + 1]

    def diagonal_block(q):
        pair = mine if q < 2 else other
        return score[pair, 512 + 128 * q : 640 + 128 * q, 128 * (q % 2) : 128 * (q % 2) + 128]

    diagonal = [
        jnp.sum(
            jnp.where(eye, diagonal_block(q), 0.0), axis=0, keepdims=True
        )
        for q in range(4)
    ]

    def spread(lse, at):
        for q in range(4):
            col_lse[at + 128 * q : at + 128 * q + 128, :] = jnp.broadcast_to(
                lse[q : q + 1, :], (128, 128)
            ).T

    to_p.wait_recv()
    lse_own = log_add(stat[0, 0:4, :], stat[1, 0:4, :])
    spread(lse_own, 512)
    to_r.wait_recv()
    row_lse[...] = log_add(stat[4], stat[5])
    loss_copy = remote(loss_own, loss_in, L_Y, to_y)
    unit = eye.astype(F32)

    def probability(p, k, q):
        at = slice(128 * q, 128 * q + 128)
        r = 2 * p + k
        scored = score[p, at, 128 * k : 128 * k + 128]
        row = row_lse[pl.ds(r, 1), :]
        value = 0.5 * (jnp.exp(scored - row) + jnp.exp(scored - col_lse[at, :]))
        if q >= 4:
            value = value - jnp.where(r == place[q - 4], unit, 0.0)
        prob[at, block(r, 128)] = value.astype(BF16)

    def own_probability(p, k):
        for q in range(4, 8):
            probability(p, k, q)

    def ahead(p, carry):
        own_probability(p, 0)
        own_probability(p, 1)
        return carry

    lax.fori_loop(0, jnp.where(first, PAIRS, 0), ahead, 0)
    to_n.wait_recv()
    spread(log_add(stat[2, 0:4, :], stat[3, 0:4, :]), 0)

    def partial(r):
        return remote(part_out.at[block(r, 128)], part_in.at[block(r, 128)], G_Y + r, to_y)

    def relay_out(p):
        r = 2 * p + 1
        return remote(part_out.at[block(r, 128)], relay_a, G_Y + r, (base + 4 - 3 * p, m), R_A)

    passed = jnp.where(place_in_half == 1, 3, 1)
    relay_in = remote(relay_a, relay_a, R_A, to_y)
    relay_over = remote(relay_a, relay_b, R_B, to_y)
    relay_back = remote(relay_b, part_in.at[block(passed, 128)], R_A, (base, m), G_Y + passed)

    def prev_probability(p, carry):
        for k in range(2):
            for q in range(4):
                probability(p, k, q)
        return carry

    def gradient(p, carry, with_prev=False):
        for k in range(2):
            if with_prev:
                for q in range(4):
                    probability(p, k, q)

            @pl.when(jnp.logical_not(first))
            def _():
                own_probability(p, k)

            lanes = block(2 * p + k, 128)
            part_out[lanes, :] = dot_tn(prob[:, lanes], text[:, 256:512]).astype(BF16)
            if k == 0:

                @pl.when(jnp.logical_not(relay & (p == 3)))
                def _():
                    partial(2 * p).start()

            else:

                @pl.when(first & (p < 2))
                def _():
                    relay_out(p).start()

                @pl.when(jnp.logical_not(first & (p < 2) | relay & (p == 3)))
                def _():
                    partial(2 * p + 1).start()

        return carry

    def visit(k):
        rows = pl.ds(256 * (k % 2), 256)
        kept = 1 - k // 2
        taken = lax.rem(kept + back_swap, 2)
        return remote(
            visit_out.at[rows, block(taken)], visit_in.at[rows, pl.ds(256 * kept, 256)], V_X + k, to_prev
        )

    def visiting(kept):
        lanes = block(lax.rem(kept + back_swap, 2))
        for rows in (slice(0, 256), slice(256, 512)):
            visit_out[rows, lanes] = dot_nn(prob[rows, :], full[:, lanes]).astype(BF16)

    gradient(0, 0, with_prev=True)
    lax.fori_loop(1, PAIRS, prev_probability, 0)
    visiting(1)
    visit(0).start()
    visit(1).start()
    gradient(1, 0)
    visiting(0)
    visit(2).start()

    @pl.when(jnp.logical_not(relay))
    def _():
        visit(3).start()

    lax.fori_loop(2, PAIRS, gradient, 0)
    for q in range(4):
        loss_own[q : q + 1, :] = (
            0.5 * (row_lse[pl.ds(place[q], 1), :] + lse_own[q : q + 1, :]) - diagonal[q]
        )
    loss_own[4:8, :] = jnp.zeros((4, 128), F32)
    loss_copy.start()

    @pl.when(relay)
    def _():
        relay_in.wait_recv()
        relay_over.start()
        partial(6).start()
        partial(7).start()

    def image_final(i, carry):
        late = jnp.where(i < 2, 2 * i, jnp.where(i < 6, i + 2, 2 * i - 11))
        r = jnp.where(first, late, i)
        lanes = block(r, 128)
        value = dot_tn(prob[:, lanes], text[:, 0:256])
        partial(r).wait_recv()
        image_out[lanes, :] = (factor * (value + part_in[lanes, :].astype(F32))).astype(BF16)
        return carry

    def text_value(k):
        rows = slice(256 * (k % 2), 256 * (k % 2) + 256)
        lanes = slice(256, 512) if k < 2 else slice(0, 256)
        own_term = dot_nn(prob[512 + rows.start : 512 + rows.stop, :], full[:, lanes])
        visit(k).wait_recv()
        return (factor * (own_term + visit_in[rows, lanes].astype(F32))).astype(BF16)

    text_copies = []
    for k in range(2):
        rows = pl.ds(256 * k, 256)
        target = text_out.at[block(mine if k == 0 else other)]
        text_copies.append(remote(text_send.at[rows], target, T_Y + k, to_y))
    lax.fori_loop(0, 4, image_final, 0)
    for k in range(2):
        text_send[256 * k : 256 * k + 256, :] = text_value(k)
        text_copies[k].start()

    @pl.when(relay)
    def _():
        relay_over.wait_recv()
        relay_back.start()
        visit(3).start()

    lax.fori_loop(4, CHUNKS, image_final, 0)
    for k in range(2):
        text_out[block(mine if k == 0 else other), :] = text_value(2 + k)

    loss_copy.wait_recv()
    loss_out[...] = jnp.where(swap == 1, loss_in[0:2, :], loss_own[0:2, :])
    for copy in sent + [loss_copy] + text_copies:
        copy.wait_send()

    @pl.when(relay)
    def _():
        relay_over.wait_send()
        relay_back.wait_send()

    for k in range(4):
        visit(k).wait_send()
    for r in range(CHUNKS):
        y_image(r).wait_send()
        c_forward(r).wait_send()
        partial(r).wait_send()
    for copy in text_copies:
        copy.wait_recv()


def finish(image_ref, text_ref, loss_ref, image_out, text_out, loss_out, loss, sem):
    copies = []
    for k in range(4):
        rows = pl.ds(256 * k, 256)
        copies.append(pltpu.make_async_copy(image_ref.at[rows], image_out.at[rows], sem.at[k]))
        copies.append(pltpu.make_async_copy(text_ref.at[rows], text_out.at[rows], sem.at[4 + k]))
    for copy in copies:
        copy.start()
    for k in range(2):
        loss[pl.ds(128 * k, 128)] = loss_ref[k, :]
    copies.append(pltpu.make_async_copy(loss, loss_out, sem.at[8]))
    copies[-1].start()
    for copy in copies:
        copy.wait()


def local(n_dp, image_emb, text_emb, logit_scale):
    vmem = pltpu.VMEM
    image_grad, text_grad, loss = pl.pallas_call(
        functools.partial(kernel, n_dp),
        out_shape=(
            vmem((1024, 256), BF16),
            vmem((1024, 256), BF16),
            vmem((2, 128), F32),
        ),
        in_specs=[
            pl.BlockSpec(memory_space=pltpu.SMEM),
            pl.BlockSpec(memory_space=pl.ANY),
            pl.BlockSpec(memory_space=pl.ANY),
        ],
        out_specs=[pl.BlockSpec(memory_space=vmem)] * 3,
        scratch_shapes=[
            vmem((1024, 1024), BF16),
            vmem((1024, 1024), BF16),
            vmem((PAIRS, 1024, 256), F32),
            vmem((2, 8, 128), F32),
            vmem((PAIRS, 8, 128), F32),
            vmem((PAIRS, 8, 128), F32),
            vmem((6, 8, 128), F32),
            vmem((8, 128), F32),
            vmem((1024, 128), F32),
            vmem((1024, 1024), BF16),
            vmem((512, 512), BF16),
            vmem((512, 512), BF16),
            vmem((1024, 256), BF16),
            vmem((1024, 256), BF16),
            vmem((512, 256), BF16),
            vmem((8, 128), F32),
            vmem((8, 128), F32),
            vmem((128, 256), BF16),
            vmem((128, 256), BF16),
            pltpu.SemaphoreType.DMA((N_COPIES,)),
            pltpu.SemaphoreType.DMA((N_COPIES,)),
            pltpu.SemaphoreType.DMA((3,)),
        ],
        compiler_params=pltpu.CompilerParams(
            collective_id=0, has_side_effects=True, vmem_limit_bytes=56 * 1024 * 1024
        ),
        cost_estimate=pl.CostEstimate(
            flops=4 * 2**31, bytes_accessed=2**21, transcendentals=2**22
        ),
    )(logit_scale, image_emb, text_emb)
    return pl.pallas_call(
        finish,
        out_shape=(
            jax.ShapeDtypeStruct((1024, 256), BF16),
            jax.ShapeDtypeStruct((1024, 256), BF16),
            jax.ShapeDtypeStruct((256,), F32),
        ),
        in_specs=[pl.BlockSpec(memory_space=vmem)] * 3,
        out_specs=[pl.BlockSpec(memory_space=pl.ANY)] * 3,
        scratch_shapes=[vmem((256,), F32), pltpu.SemaphoreType.DMA((9,))],
    )(*(pltpu.with_memory_space_constraint(x, vmem) for x in (image_grad, text_grad, loss)))


def solution(mesh):
    return jax.shard_map(
        functools.partial(local, mesh.shape["dp"]),
        mesh=mesh,
        in_specs=(P("dp", "mp"), P("dp", "mp"), P()),
        out_specs=(P("dp", "mp"), P("dp", "mp"), P(("dp", "mp"))),
        check_vma=False,
    )
```

```python
import functools

import jax
import jax.numpy as jnp
from jax import lax
from jax.experimental import pallas as pl
from jax.experimental.pallas import tpu as pltpu
from jax.sharding import PartitionSpec as P

MESH = pl.DeviceIdType.MESH
F32 = jnp.float32
BF16 = jnp.bfloat16
CHUNKS = 8
PAIRS = 4

Y_T = 0
Y_I = 4
C_I = 12
C_T = 13
C_V = 15
X_T = 19
X_V = 23
C_P = 27
C_F = 31
S_R = 39
S_N = 40
S_P = 41
V_X = 42
G_Y = 46
T_Y = 54
L_Y = 58
R_A = 59
R_B = 60
N_COPIES = 61


def dot_nt(a, b):
    return lax.dot_general(a, b, (((1,), (1,)), ((), ())), preferred_element_type=F32)


def dot_tn(a, b):
    return lax.dot_general(a, b, (((0,), (0,)), ((), ())), preferred_element_type=F32)


def dot_nn(a, b):
    return lax.dot_general(a, b, (((1,), (0,)), ((), ())), preferred_element_type=F32)


def log_add(a, b):
    top = jnp.maximum(a, b)
    return top + jnp.log(jnp.exp(a - top) + jnp.exp(b - top))


def kernel(
    n_dp,
    factor_ref,
    image_ref,
    text_ref,
    image_out,
    text_out,
    loss_out,
    full,
    text,
    score,
    row_part,
    col_max,
    col_sum,
    stat,
    row_lse,
    col_lse,
    prob,
    visit_out,
    visit_in,
    part_out,
    part_in,
    text_send,
    loss_own,
    loss_in,
    relay_a,
    relay_b,
    send_sem,
    recv_sem,
    local_sem,
):
    d = lax.axis_index("dp")
    m = lax.axis_index("mp")
    c_m = m + 1 - 2 * lax.rem(m, 2)
    y_m = lax.rem(m + 2, 4)
    nxt = lax.rem(d + 1, n_dp)
    prv = lax.rem(d + n_dp - 1, n_dp)
    half = n_dp // 2
    swap = lax.div(d, half)
    out_swap = lax.div(lax.rem(d, half) + 1, half)
    back_swap = 1 - lax.div(lax.rem(d, half) + half - 1, half)
    to_c, to_y = (d, c_m), (d, y_m)
    to_next = (nxt, lax.rem(m + 2 * out_swap, 4))
    to_prev = (prv, lax.rem(m + 2 * back_swap, 4))
    place_in_half = lax.rem(d, half)
    first = place_in_half == 0
    relay = (place_in_half == 1) | (place_in_half == 4)
    base = d - place_in_half
    last = place_in_half == half - 1
    mine = lax.rem(m + 2 * swap, 4)
    other = lax.rem(c_m + 2 * swap, 4)
    mine_y = lax.rem(mine + 2, 4)
    other_y = lax.rem(other + 2, 4)

    def block(index, size=256):
        return pl.ds(pl.multiple_of(index * size, size), size)

    def remote(src, dst, index, device, arrival=None):
        return pltpu.make_async_remote_copy(
            src_ref=src,
            dst_ref=dst,
            send_sem=send_sem.at[index],
            recv_sem=recv_sem.at[index if arrival is None else arrival],
            device_id=device,
            device_id_type=MESH,
        )

    own, via = pl.ds(0, 256), pl.ds(256, 256)

    def piece(first, second, k):
        return block(2 * (first if k < 2 else second) + k % 2, 128)

    locals_ = [
        pltpu.make_async_copy(image_ref, full.at[:, own], local_sem.at[0]),
        pltpu.make_async_copy(text_ref.at[block(mine)], text.at[pl.ds(512, 256), own], local_sem.at[1]),
        pltpu.make_async_copy(text_ref.at[block(other)], text.at[pl.ds(768, 256), own], local_sem.at[2]),
    ]
    barrier = pltpu.get_barrier_semaphore()
    for device in (to_c, to_y, to_prev):
        pl.semaphore_signal(barrier, inc=1, device_id=device, device_id_type=MESH)

    @pl.when(place_in_half == 4)
    def _():
        pl.semaphore_signal(barrier, inc=1, device_id=(base, m), device_id_type=MESH)

    for copy in locals_:
        copy.start()

    @pl.when(first)
    def _():
        pl.semaphore_wait(barrier, 4)

    @pl.when(jnp.logical_not(first))
    def _():
        pl.semaphore_wait(barrier, 3)


    y_text = [
        remote(text_ref.at[piece(mine_y, other_y, k)], text.at[pl.ds(512 + 128 * k, 128), via], Y_T + k, to_y)
        for k in range(4)
    ]
    c_image = remote(image_ref, full.at[:, pl.ds(512, 256)], C_I, to_c)
    c_text = [
        remote(text_ref.at[block(other)], text.at[pl.ds(512, 256), pl.ds(512, 256)], C_T, to_c),
        remote(text_ref.at[block(mine)], text.at[pl.ds(768, 256), pl.ds(512, 256)], C_T + 1, to_c),
    ]
    c_via = [
        remote(
            text.at[pl.ds(512 + 128 * k, 128), via],
            text.at[pl.ds(512 + 128 * ((k + 2) % 4), 128), pl.ds(768, 256)],
            C_V + k,
            to_c,
        )
        for k in range(4)
    ]
    x_own = [
        remote(text_ref.at[piece(mine, other, k)], text.at[pl.ds(128 * k, 128), block(out_swap)], X_T + k, to_next)
        for k in range(4)
    ]
    x_via = [
        remote(
            text.at[pl.ds(512 + 128 * k, 128), via],
            text.at[pl.ds(128 * k, 128), block(1 - out_swap)],
            X_V + k,
            to_next,
        )
        for k in range(4)
    ]
    c_prev = [
        remote(
            text.at[pl.ds(128 * k, 128), pl.ds(0, 512)],
            text.at[pl.ds(128 * ((k + 2) % 4), 128), pl.ds(512, 512)],
            C_P + k,
            to_c,
        )
        for k in range(4)
    ]

    def y_image(r):
        return remote(image_ref.at[block(r, 128)], full.at[block(r, 128), via], Y_I + r, to_y)

    def c_forward(r):
        return remote(full.at[block(r, 128), via], full.at[block(r, 128), pl.ds(768, 256)], C_F + r, to_c)

    for k in range(4):
        y_text[k].start()
    for k in range(4):
        x_own[k].start()
    c_text[0].start()
    c_text[1].start()
    c_image.start()
    for r in range(CHUNKS):
        y_image(r).start()

    for k in range(4):
        y_text[k].wait_recv()
        x_via[k].start()
        c_via[k].start()
    for copy in locals_:
        copy.wait()
    for copy in [c_image] + c_text + c_via:
        copy.wait_recv()
    sent = y_text + [c_image] + c_text + c_via + x_own + x_via + c_prev

    factor = factor_ref[0]
    eye = lax.broadcasted_iota(jnp.int32, (128, 128), 0) == lax.broadcasted_iota(
        jnp.int32, (128, 128), 1
    )

    def arrive(p, rows):
        for r in (2 * p, 2 * p + 1):
            y_image(r).wait_recv()
            c_forward(r).start()
        scored = dot_nt(text[rows, 0:768], full[block(p), 0:768])
        for r in (2 * p, 2 * p + 1):
            c_forward(r).wait_recv()
        return factor * (scored + dot_nt(text[rows, 768:1024], full[block(p), 768:1024]))

    def statistics(t, p, scored):
        score[p, 512 * t : 512 * t + 512, :] = scored
        top = jnp.max(scored, axis=0, keepdims=True)
        total = top + jnp.log(jnp.sum(jnp.exp(scored - top), axis=0, keepdims=True))
        for k in range(2):
            row_part[t, pl.ds(2 * p + k, 1), :] = total[:, 128 * k : 128 * k + 128]
        highest = jnp.max(scored, axis=1, keepdims=True)
        summed = jnp.sum(jnp.exp(scored - highest), axis=1, keepdims=True)
        for q in range(4):
            at = slice(128 * q, 128 * q + 128)
            col_max[p, 4 * t + q : 4 * t + q + 1, :] = jnp.sum(
                jnp.where(eye, highest[at], 0.0), axis=0, keepdims=True
            )
            col_sum[p, 4 * t + q : 4 * t + q + 1, :] = jnp.sum(
                jnp.where(eye, summed[at], 0.0), axis=0, keepdims=True
            )

    def own_chunk(p, carry):
        statistics(1, p, arrive(p, slice(512, 1024)))
        return carry

    def prev_chunk(p, carry):
        statistics(0, p, factor * dot_nt(text[0:512, :], full[block(p), :]))
        return carry

    def column(t):
        rows = slice(4 * t, 4 * t + 4)
        top = col_max[0, rows, :]
        for p in range(1, PAIRS):
            top = jnp.maximum(top, col_max[p, rows, :])
        total = jnp.zeros_like(top)
        for p in range(PAIRS):
            total = total + col_sum[p, rows, :] * jnp.exp(col_max[p, rows, :] - top)
        at = 2 - 2 * t
        stat[at, 0:4, :] = top + jnp.log(total)
        stat[at, 4:8, :] = jnp.zeros((4, 128), F32)

    to_n = remote(stat.at[0], stat.at[3], S_N, to_next)
    to_p = remote(stat.at[2], stat.at[1], S_P, to_prev)
    to_r = remote(stat.at[4], stat.at[5], S_R, to_y)

    early = jnp.where(first | last, PAIRS, 2)
    later = jnp.where(first | last, PAIRS, 3)
    lax.fori_loop(0, early, own_chunk, 0)

    @pl.when(first | last)
    def _():
        column(1)
        to_n.start()

    for k in range(4):
        x_own[k].wait_recv()
        x_via[k].wait_recv()
        c_prev[k].start()
    for k in range(4):
        c_prev[k].wait_recv()
    lax.fori_loop(0, early, prev_chunk, 0)
    lax.fori_loop(early, later, own_chunk, 0)
    lax.fori_loop(early, later, prev_chunk, 0)

    @pl.when(jnp.logical_not(first | last))
    def _():
        both = arrive(PAIRS - 1, slice(0, 1024))
        statistics(1, PAIRS - 1, both[512:1024, :])
        column(1)
        to_n.start()
        statistics(0, PAIRS - 1, both[0:512, :])

    stat[4] = log_add(row_part[0], row_part[1])
    to_r.start()
    column(0)
    to_p.start()
    sent += [to_n, to_p, to_r]

    place = [2 * mine, 2 * mine + 1, 2 * other, 2 * other + 1]

    def diagonal_block(q):
        pair = mine if q < 2 else other
        return score[pair, 512 + 128 * q : 640 + 128 * q, 128 * (q % 2) : 128 * (q % 2) + 128]

    diagonal = [
        jnp.sum(
            jnp.where(eye, diagonal_block(q), 0.0), axis=0, keepdims=True
        )
        for q in range(4)
    ]

    def spread(lse, at):
        for q in range(4):
            col_lse[at + 128 * q : at + 128 * q + 128, :] = jnp.broadcast_to(
                lse[q : q + 1, :], (128, 128)
            ).T

    to_p.wait_recv()
    lse_own = log_add(stat[0, 0:4, :], stat[1, 0:4, :])
    spread(lse_own, 512)
    to_r.wait_recv()
    row_lse[...] = log_add(stat[4], stat[5])
    loss_copy = remote(loss_own, loss_in, L_Y, to_y)
    unit = eye.astype(F32)

    def probability(p, k, q):
        at = slice(128 * q, 128 * q + 128)
        r = 2 * p + k
        scored = score[p, at, 128 * k : 128 * k + 128]
        row = row_lse[pl.ds(r, 1), :]
        value = 0.5 * (jnp.exp(scored - row) + jnp.exp(scored - col_lse[at, :]))
        if q >= 4:
            value = value - jnp.where(r == place[q - 4], unit, 0.0)
        prob[at, block(r, 128)] = value.astype(BF16)

    def own_probability(p, k):
        for q in range(4, 8):
            probability(p, k, q)

    def ahead(p, carry):
        own_probability(p, 0)
        own_probability(p, 1)
        return carry

    lax.fori_loop(0, jnp.where(first, PAIRS, 0), ahead, 0)
    to_n.wait_recv()
    spread(log_add(stat[2, 0:4, :], stat[3, 0:4, :]), 0)

    def partial(r):
        return remote(part_out.at[block(r, 128)], part_in.at[block(r, 128)], G_Y + r, to_y)

    def relay_out(p):
        r = 2 * p + 1
        return remote(part_out.at[block(r, 128)], relay_a, G_Y + r, (base + 4 - 3 * p, m), R_A)

    passed = jnp.where(place_in_half == 1, 3, 1)
    relay_in = remote(relay_a, relay_a, R_A, to_y)
    relay_over = remote(relay_a, relay_b, R_B, to_y)
    relay_back = remote(relay_b, part_in.at[block(passed, 128)], R_A, (base, m), G_Y + passed)

    def prev_probability(p, carry):
        for k in range(2):
            for q in range(4):
                probability(p, k, q)
        return carry

    def gradient(p, carry, with_prev=False):
        for k in range(2):
            if with_prev:
                for q in range(4):
                    probability(p, k, q)

            @pl.when(jnp.logical_not(first))
            def _():
                own_probability(p, k)

            lanes = block(2 * p + k, 128)
            part_out[lanes, :] = dot_tn(prob[:, lanes], text[:, 256:512]).astype(BF16)
            if k == 0:

                @pl.when(jnp.logical_not(relay & (p == 3)))
                def _():
                    partial(2 * p).start()

            else:

                @pl.when(first & (p < 2))
                def _():
                    relay_out(p).start()

                @pl.when(jnp.logical_not(first & (p < 2) | relay & (p == 3)))
                def _():
                    partial(2 * p + 1).start()

        return carry

    def visit(k):
        rows = pl.ds(256 * (k % 2), 256)
        kept = 1 - k // 2
        taken = lax.rem(kept + back_swap, 2)
        return remote(
            visit_out.at[rows, block(taken)], visit_in.at[rows, pl.ds(256 * kept, 256)], V_X + k, to_prev
        )

    def visiting(kept):
        lanes = block(lax.rem(kept + back_swap, 2))
        for rows in (slice(0, 256), slice(256, 512)):
            visit_out[rows, lanes] = dot_nn(prob[rows, :], full[:, lanes]).astype(BF16)

    gradient(0, 0, with_prev=True)
    lax.fori_loop(1, PAIRS, prev_probability, 0)
    visiting(1)
    visit(0).start()
    visit(1).start()
    gradient(1, 0)
    visiting(0)
    visit(2).start()

    @pl.when(jnp.logical_not(relay))
    def _():
        visit(3).start()

    lax.fori_loop(2, PAIRS, gradient, 0)
    for q in range(4):
        loss_own[q : q + 1, :] = (
            0.5 * (row_lse[pl.ds(place[q], 1), :] + lse_own[q : q + 1, :]) - diagonal[q]
        )
    loss_own[4:8, :] = jnp.zeros((4, 128), F32)
    loss_copy.start()

    @pl.when(relay)
    def _():
        relay_in.wait_recv()
        relay_over.start()
        partial(6).start()
        partial(7).start()

    def image_final(i, carry):
        late = jnp.where(i < 2, 2 * i, jnp.where(i < 6, i + 2, 2 * i - 11))
        r = jnp.where(first, late, i)
        lanes = block(r, 128)
        value = dot_tn(prob[:, lanes], text[:, 0:256])
        partial(r).wait_recv()
        image_out[lanes, :] = (factor * (value + part_in[lanes, :].astype(F32))).astype(BF16)
        return carry

    def text_value(k):
        rows = slice(256 * (k % 2), 256 * (k % 2) + 256)
        lanes = slice(256, 512) if k < 2 else slice(0, 256)
        own_term = dot_nn(prob[512 + rows.start : 512 + rows.stop, :], full[:, lanes])
        visit(k).wait_recv()
        return (factor * (own_term + visit_in[rows, lanes].astype(F32))).astype(BF16)

    text_copies = []
    for k in range(2):
        rows = pl.ds(256 * k, 256)
        target = text_out.at[block(mine if k == 0 else other)]
        text_copies.append(remote(text_send.at[rows], target, T_Y + k, to_y))
    lax.fori_loop(0, 4, image_final, 0)
    for k in range(2):
        text_send[256 * k : 256 * k + 256, :] = text_value(k)
        text_copies[k].start()

    @pl.when(relay)
    def _():
        relay_over.wait_recv()
        relay_back.start()
        visit(3).start()

    lax.fori_loop(4, CHUNKS, image_final, 0)
    for k in range(2):
        text_out[block(mine if k == 0 else other), :] = text_value(2 + k)

    loss_copy.wait_recv()
    loss_out[...] = jnp.where(swap == 1, loss_in[0:2, :], loss_own[0:2, :])
    for copy in sent + [loss_copy] + text_copies:
        copy.wait_send()

    @pl.when(relay)
    def _():
        relay_over.wait_send()
        relay_back.wait_send()

    for k in range(4):
        visit(k).wait_send()
    for r in range(CHUNKS):
        y_image(r).wait_send()
        c_forward(r).wait_send()
        partial(r).wait_send()
    for copy in text_copies:
        copy.wait_recv()


def finish(image_ref, text_ref, loss_ref, image_out, text_out, loss_out, loss, sem):
    copies = [
        pltpu.make_async_copy(image_ref, image_out, sem.at[0]),
        pltpu.make_async_copy(text_ref, text_out, sem.at[1]),
    ]
    for copy in copies:
        copy.start()
    for k in range(2):
        loss[pl.ds(128 * k, 128)] = loss_ref[k, :]
    copies.append(pltpu.make_async_copy(loss, loss_out, sem.at[2]))
    copies[-1].start()
    for copy in copies:
        copy.wait()


def local(n_dp, image_emb, text_emb, logit_scale):
    vmem = pltpu.VMEM
    image_grad, text_grad, loss = pl.pallas_call(
        functools.partial(kernel, n_dp),
        out_shape=(
            vmem((1024, 256), BF16),
            vmem((1024, 256), BF16),
            vmem((2, 128), F32),
        ),
        in_specs=[
            pl.BlockSpec(memory_space=pltpu.SMEM),
            pl.BlockSpec(memory_space=pl.ANY),
            pl.BlockSpec(memory_space=pl.ANY),
        ],
        out_specs=[pl.BlockSpec(memory_space=vmem)] * 3,
        scratch_shapes=[
            vmem((1024, 1024), BF16),
            vmem((1024, 1024), BF16),
            vmem((PAIRS, 1024, 256), F32),
            vmem((2, 8, 128), F32),
            vmem((PAIRS, 8, 128), F32),
            vmem((PAIRS, 8, 128), F32),
            vmem((6, 8, 128), F32),
            vmem((8, 128), F32),
            vmem((1024, 128), F32),
            vmem((1024, 1024), BF16),
            vmem((512, 512), BF16),
            vmem((512, 512), BF16),
            vmem((1024, 256), BF16),
            vmem((1024, 256), BF16),
            vmem((512, 256), BF16),
            vmem((8, 128), F32),
            vmem((8, 128), F32),
            vmem((128, 256), BF16),
            vmem((128, 256), BF16),
            pltpu.SemaphoreType.DMA((N_COPIES,)),
            pltpu.SemaphoreType.DMA((N_COPIES,)),
            pltpu.SemaphoreType.DMA((3,)),
        ],
        compiler_params=pltpu.CompilerParams(
            collective_id=0, has_side_effects=True, vmem_limit_bytes=56 * 1024 * 1024
        ),
        cost_estimate=pl.CostEstimate(
            flops=4 * 2**31, bytes_accessed=2**21, transcendentals=2**22
        ),
    )(logit_scale, image_emb, text_emb)
    return pl.pallas_call(
        finish,
        out_shape=(
            jax.ShapeDtypeStruct((1024, 256), BF16),
            jax.ShapeDtypeStruct((1024, 256), BF16),
            jax.ShapeDtypeStruct((256,), F32),
        ),
        in_specs=[pl.BlockSpec(memory_space=vmem)] * 3,
        out_specs=[pl.BlockSpec(memory_space=pl.ANY)] * 3,
        scratch_shapes=[vmem((256,), F32), pltpu.SemaphoreType.DMA((3,))],
    )(*(pltpu.with_memory_space_constraint(x, vmem) for x in (image_grad, text_grad, loss)))


def solution(mesh):
    return jax.shard_map(
        functools.partial(local, mesh.shape["dp"]),
        mesh=mesh,
        in_specs=(P("dp", "mp"), P("dp", "mp"), P()),
        out_specs=(P("dp", "mp"), P("dp", "mp"), P(("dp", "mp"))),
        check_vma=False,
    )
```
